256 devices in a mesh: dp: 16 (over x_hi, z), seq: 16 (over y, x_lo, core).
Axes of the slice: x: 4 (x_hi: 2, x_lo: 2; x = x_hi * 2 + x_lo), y: 4, z: 8, core: 2. Of those that a mesh axis runs over, the one named last changes fastest.
Arguments:
- tokens: bfloat16 [32, 1024, 2240], P('dp', 'seq'), may hold values from -8 to 8
- q_raw: bfloat16 [32, 1024, 1120], P('dp', 'seq'), may hold values from -6 to 6
- k_raw: bfloat16 [32, 1024, 1120], P('dp', 'seq'), may hold values from -6 to 6
- w_value: bfloat16 [2240, 1120], P('dp'), may hold values from -0.125 to 0.125
- w_out: bfloat16 [1120, 2240], P('dp'), may hold values from -0.1875 to 0.1875
- cotangent: bfloat16 [32, 1024, 2240], P('dp', 'seq'), may hold values from -6 to 6
Outputs:
- att_output: bfloat16 [32, 1024, 2240], P('dp', 'seq')
- grad_tokens: bfloat16 [32, 1024, 2240], P('dp', 'seq')
- grad_query: bfloat16 [32, 1024, 1120], P('dp', 'seq')
- grad_key: bfloat16 [32, 1024, 1120], P('dp', 'seq')
- grad_value_w: float32 [2240, 1120], P('dp', 'seq')
- grad_out_w: float32 [1120, 2240], P('dp', 'seq')
The draws below stay inside these ranges and needn't reach their ends.
All inputs are finite; a program needn't handle non-finite values.
Results may differ from the reference program's by a relative error of at most 0.005.
Values may be sent and summed in bfloat16 or wider, within the bound.
A program may use at most 128 MiB of HBM per device.

```python
import jax
import jax.numpy as jnp
from jax import lax

D = 2240
HEADS = 35
HS = 32
LAT = 32
HD = 1120
NTOK = 1024
IMAGES = 32


def draw_tokens(key, part):
    key = jax.random.fold_in(key, 11)
    row_key, cell_key = jax.random.split(key, 2)
    row_part = 1.5 * jax.random.normal(row_key, (IMAGES, LAT, 1, D), jnp.float32)
    cell_part = 0.7 * jax.random.normal(cell_key, (IMAGES, LAT, LAT, D), jnp.float32)
    mixed_rows = row_part + cell_part
    return jnp.clip(mixed_rows, -8.0, 8.0).reshape(IMAGES, LAT * LAT, D).astype(jnp.bfloat16)


def raised(result, key, source, target, parts, factor):
    def block_of(axis_at):
        return (jnp.arange(result.shape[axis_at]) // (result.shape[axis_at] // parts)).reshape((-1,) + (1,) * (result.ndim - 1 - axis_at))

    near = jax.random.permutation(key, parts)[block_of(target)]
    second = (block_of(target) + parts // 2) % parts
    return jnp.where((block_of(source) == near) | (block_of(source) == second), factor * result, result)


def steps_of(own_key, extent, shards, smallest, top_value):
    def one(position, blocks):
        steps = jax.random.uniform(jax.random.fold_in(jax.random.fold_in(own_key, 6), position), (blocks,), jnp.float32, smallest / len(shards), top_value / len(shards))
        return jnp.repeat(jnp.exp(steps), extent[position] // blocks).reshape((-1,) + (1,) * (len(extent) - position - 1))

    gain = one(*shards[0])
    for cut in shards[1:]:
        gain = gain * one(*cut)
    return gain


def normal_values(key, extent, deviation, reach, cuts=(), dtype=jnp.bfloat16):
    level = steps_of(key, extent, cuts, -0.22, 0.18) if cuts else 1.0
    drawn = jax.random.normal(key, extent, jnp.float32) * deviation * level
    return jnp.minimum(jnp.maximum(drawn, -reach), reach).astype(dtype)


def heavy_noise(own_key, dims, spread, reach, pieces, heavy, kind=jnp.bfloat16):
    result = spread * jax.random.normal(own_key, dims, jnp.float32)
    if pieces:
        result = result * steps_of(own_key, dims, pieces, -0.22, 0.18)
    return jnp.clip(raised(result, jax.random.fold_in(own_key, 3), *heavy), -reach, reach).astype(kind)


def setup_inputs(seed: int = 0) -> dict:
    splits = jax.random.split(jax.random.key(seed), 7)
    return {
        "tokens": draw_tokens(jax.random.fold_in(splits[6], 71), 0),
        "q_raw": normal_values(splits[1], (IMAGES, NTOK, HD), 1.0, 6.0, ((0, 16), (1, 16))),
        "k_raw": normal_values(splits[2], (IMAGES, NTOK, HD), 1.0, 6.0, ((0, 16), (1, 16))),
        "w_value": normal_values(splits[3], (D, HD), D ** -0.5, 0.125, ((0, 16),)),
        "w_out": normal_values(splits[4], (HD, D), HD ** -0.5, 0.1875, ((0, 16),)),
        "cotangent": heavy_noise(splits[5], (IMAGES, NTOK, D), 1.0, 6.0, ((0, 16), (1, 16)), (1, 2, 16, 2.0)),
    }


def reference(tokens, q_raw, k_raw, w_value, w_out, cotangent):
    images = tokens.shape[0]
    tok_count = tokens.shape[1]
    high = lax.Precision.HIGHEST
    flat_rows = tokens.reshape(images * tok_count, D)
    values = jnp.dot(flat_rows, w_value, preferred_element_type=jnp.float32).astype(jnp.bfloat16)
    values_f = values.astype(jnp.float32).reshape(images, tok_count, HEADS, HS)
    feat_query = jnp.maximum(q_raw, 0).astype(jnp.float32).reshape(images, tok_count, HEADS, HS)
    feat_key = jnp.maximum(k_raw, 0).astype(jnp.float32).reshape(images, tok_count, HEADS, HS)
    kv_state = jnp.einsum("bnhd,bnhe->bhde", feat_key, values_f, precision=high)
    key_total = jnp.sum(feat_key, axis=1)
    numer = jnp.einsum("bnhd,bhde->bnhe", feat_query, kv_state, precision=high)
    denom = jnp.einsum("bnhd,bhd->bnh", feat_query, key_total, precision=high) + 1.0
    att_ratio = numer / denom[..., None]
    att_heads = att_ratio.astype(jnp.bfloat16).reshape(images * tok_count, HD)
    att_output = jnp.dot(att_heads, w_out, preferred_element_type=jnp.float32).astype(jnp.bfloat16)
    cot_rows = cotangent.reshape(images * tok_count, D)
    grad_heads = jnp.dot(cot_rows, w_out.T, preferred_element_type=jnp.float32)
    grad_out_w = jnp.dot(att_heads.T, cot_rows, preferred_element_type=jnp.float32)
    grad_numer = grad_heads.reshape(images, tok_count, HEADS, HS) / denom[..., None]
    grad_denom = -jnp.sum(grad_numer * att_ratio, axis=-1)
    query_part = jnp.einsum("bnhe,bhde->bnhd", grad_numer, kv_state, precision=high)
    query_part = query_part + grad_denom[..., None] * key_total[:, None]
    grad_query = jnp.where(q_raw > 0, query_part.reshape(images, tok_count, HD), 0.0).astype(jnp.bfloat16)
    grad_state = jnp.einsum("bnhd,bnhe->bhde", feat_query, grad_numer, precision=high)
    grad_total = jnp.einsum("bnhd,bnh->bhd", feat_query, grad_denom, precision=high)
    grad_values = jnp.einsum("bnhd,bhde->bnhe", feat_key, grad_state, precision=high).astype(jnp.bfloat16)
    key_part = jnp.einsum("bnhe,bhde->bnhd", values_f, grad_state, precision=high) + grad_total[:, None]
    grad_key = jnp.where(k_raw > 0, key_part.reshape(images, tok_count, HD), 0.0).astype(jnp.bfloat16)
    grad_rows = grad_values.reshape(images * tok_count, HD)
    grad_tokens = jnp.dot(grad_rows, w_value.T, preferred_element_type=jnp.float32).astype(jnp.bfloat16)
    grad_value_w = jnp.dot(flat_rows.T, grad_rows, preferred_element_type=jnp.float32)
    return (att_output.reshape(images, tok_count, D), grad_tokens.reshape(images, tok_count, D), grad_query, grad_key, grad_value_w, grad_out_w)
```

```python
import jax
import jax.numpy as jnp
from jax import lax
from jax.experimental import pallas as pl
from jax.experimental.pallas import tpu as pltpu
from jax.sharding import PartitionSpec as P

BF = jnp.bfloat16
F32 = jnp.float32
MESH = pl.DeviceIdType.MESH
VM = pltpu.VMEM
SIZE = {"x": 4, "y": 4, "z": 8}
ORDERS = (("x", "y", "z"), ("y", "z", "x"), ("z", "x", "y"))
PAIRS = ((0, 1), (1, 0), (1, 1), (2, 0), (2, 1), (3, 0), (3, 1))
N_SEMS = 320


class Place:
    def __init__(self):
        dp = lax.axis_index("dp")
        seq = lax.axis_index("seq")
        self.z = lax.rem(dp, 8)
        self.y = lax.div(seq, 4)
        self.xl = lax.rem(lax.div(seq, 2), 2)
        self.c = lax.rem(seq, 2)
        self.x = lax.div(dp, 8) * 2 + self.xl
        self.p = self.y * 2 + self.xl

    def step(self, d, k):
        return lax.rem(getattr(self, d) + (k % SIZE[d]), SIZE[d])

    def dev(self, x=None, y=None, z=None, c=None):
        x = self.x if x is None else x
        y = self.y if y is None else y
        z = self.z if z is None else z
        c = self.c if c is None else c
        return (lax.div(x, 2) * 8 + z, (y * 2 + lax.rem(x, 2)) * 2 + c)

    def peer(self, d, k):
        return self.dev(**{d: self.step(d, k)})

    def sibling(self):
        return self.dev(c=1 - self.c)

    def row_peer(self, dy, dx):
        xl = lax.rem(self.xl + dx, 2)
        return self.dev(y=self.step("y", dy), x=self.x - self.xl + xl)

    def index(self, o, open_, d, b, half=None):
        co = {"x": self.x, "y": self.y, "z": self.z}
        for e in open_:
            co[e] = None
        co[d] = b
        every = slice(None)
        x = co["x"]
        xh, xl = (every, every) if x is None else (lax.div(x, 2), lax.rem(x, 2))
        z = every if co["z"] is None else co["z"]
        y = every if co["y"] is None else co["y"]
        out = (xh, z, y, xl, o)
        return out if half is None else out + (half,)


class Wire:
    def __init__(self, sems):
        self.sems = sems
        self.started = []

    def send(self, src, dst, dev):
        k = len(self.started)
        cp = pltpu.make_async_remote_copy(
            src_ref=src,
            dst_ref=dst,
            send_sem=self.sems.at[0, k],
            recv_sem=self.sems.at[1, k],
            device_id=dev,
            device_id_type=MESH,
        )
        cp.start()
        self.started.append(cp)
        return cp

    def drain(self):
        for cp in self.started:
            cp.wait_send()


def gather(wire, me, buf, o):
    open_ = []
    sib = []

    def piece(d, b, half=None):
        return buf.at[(me.c,) + me.index(o, open_, d, b, half)]

    def share(d, b, half=None):
        ref = piece(d, b, half)
        sib.append(wire.send(ref, ref, me.sibling()))

    for n, d in enumerate(ORDERS[o]):
        last = n == 2
        if last:
            share(d, getattr(me, d))
        if d != "z":
            own = piece(d, getattr(me, d))
            cps = [wire.send(own, own, me.peer(d, k)) for k in range(1, SIZE[d])]
            yield
            for k, cp in enumerate(cps, 1):
                cp.wait_recv()
                if last:
                    share(d, me.step(d, -k))
        else:
            for s in range(1, 5):
                hp, hm = (0, 1) if s == 4 else (None, None)
                fp = piece(d, me.step(d, -(s - 1)), hp)
                fm = piece(d, me.step(d, s - 1), hm)
                plus = wire.send(fp, fp, me.peer(d, 1))
                minus = wire.send(fm, fm, me.peer(d, -1))
                yield
                plus.wait_recv()
                minus.wait_recv()
                if last:
                    share(d, me.step(d, -s), hp)
                    share(d, me.step(d, s), hm)
        open_.append(d)
    yield
    for cp in sib:
        cp.wait_recv()


def scatter(wire, me, buf, o, rx, fin):
    rx = iter(rx)
    dims = ORDERS[o]
    for n, d in enumerate(dims):
        open_ = dims[n + 1 :]
        last = n == 2

        def at(k, half=None):
            return me.index(o, open_, d, me.step(d, k), half)

        own = at(0)
        if d != "z":
            slots = [next(rx) for _ in range(3)]
            cps = [
                wire.send(buf.at[at(k)], slots[k - 1], me.peer(d, k)) for k in (1, 2, 3)
            ]
            yield
            acc = buf[own].astype(F32)
            for k in range(3):
                cps[k].wait_recv()
                acc = acc + slots[k][...].astype(F32)
        else:
            up = [next(rx) for _ in range(4)]
            down = [next(rx) for _ in range(4)]
            for s in range(1, 5):
                k = 5 - s
                hp, hm = (0, 1) if s == 1 else (None, None)
                if s > 1:
                    plus.wait_recv()
                    minus.wait_recv()
                    for sign, slot, half in ((1, up[s - 2], 0), (-1, down[s - 2], 1)):
                        i = at(sign * k, half if s == 2 else None)
                        buf[i] = (buf[i].astype(F32) + slot[...].astype(F32)).astype(BF)
                plus = wire.send(buf.at[at(k, hp)], up[s - 1], me.peer(d, 1))
                minus = wire.send(buf.at[at(-k, hm)], down[s - 1], me.peer(d, -1))
                yield
            plus.wait_recv()
            minus.wait_recv()
            acc = buf[own].astype(F32) + up[3][...].astype(F32) + down[3][...].astype(F32)
        if last:
            fin[me.c, me.p, o] = acc
        else:
            buf[own] = acc.astype(BF)


def scatter_slots(o):
    dims = ORDERS[o]
    out = []
    for n, d in enumerate(dims):
        open_ = dims[n + 1 :]
        shape = ()
        if "x" in open_:
            shape += (2,)
        if "z" in open_:
            shape += (8,)
        if "y" in open_:
            shape += (4,)
        if "x" in open_:
            shape += (2,)
        tile = (16, 128)
        if d != "z":
            out += [VM(shape + (2,) + tile, BF)] * 3
        else:
            out += ([VM(shape + tile, BF)] + [VM(shape + (2,) + tile, BF)] * 3) * 2
    return out


def spread(wire, me, fin):
    mine = fin.at[me.c, me.p]
    cps = [wire.send(mine, mine, me.row_peer(dy, dx)) for dy, dx in PAIRS]
    yield
    for cp in cps:
        cp.wait_recv()
    half = fin.at[me.c]
    cp = wire.send(half, half, me.sibling())
    yield
    cp.wait_recv()


def seq_sum(wire, me, part, from_sib, from_row, total):
    cp = wire.send(part.at[1 - me.c], from_sib, me.sibling())
    yield
    cp.wait_recv()
    part[me.c] = part[me.c] + from_sib[...]
    cps = []
    for n, (dy, dx) in enumerate(PAIRS):
        p = me.step("y", dy) * 2 + lax.rem(me.xl + dx, 2)
        cps.append(
            wire.send(part.at[me.c, pl.ds(6 * p, 6)], from_row.at[n], me.row_peer(dy, dx))
        )
    yield
    acc = part[me.c, pl.ds(6 * me.p, 6)]
    for n, cp in enumerate(cps):
        cp.wait_recv()
        acc = acc + from_row[n]
    total[me.c, pl.ds(6 * me.p, 6)] = acc
    mine = total.at[me.c, pl.ds(6 * me.p, 6)]
    cps = [wire.send(mine, mine, me.row_peer(dy, dx)) for dy, dx in PAIRS]
    yield
    for cp in cps:
        cp.wait_recv()
    half = total.at[me.c]
    cp = wire.send(half, half, me.sibling())
    yield
    cp.wait_recv()


def step(gens):
    for g in list(gens):
        try:
            next(g)
        except StopIteration:
            gens.remove(g)


def split(a):
    hi = a.astype(BF)
    return hi, (a - hi.astype(F32)).astype(BF)


def dot(a, b):
    return jnp.dot(a, b, preferred_element_type=F32)


def dot_t(a, b):
    return lax.dot_general(a, b, (((1,), (1,)), ((), ())), preferred_element_type=F32)


def t_dot(a, b):
    return lax.dot_general(a, b, (((0,), (0,)), ((), ())), preferred_element_type=F32)


def fold(m):
    return m[0:32] + m[32:64] + m[64:96] + m[96:128]


def kernel(
    tok, q_in, k_in, wv_in, wo_in, cot,
    out_o, gtok_o, gq_o, gk_o, gwv_o, gwo_o,
    sems, wv, wo, wvp, wop, tokp, tok_t, cotp, qp, kp, val, attf, denf, att_h, att_p, att_t,
    ghp, gvp, gqp, gkp, part1, part2, sib1, sib2, row1, row2, tot1, tot2,
    rs_v, rs_o, fin_v, fin_o, *slots,
):
    me = Place()
    wire = Wire(sems)
    per = [len(scatter_slots(o)) for o in range(3)]
    cut = [0]
    for n in per * 2:
        cut.append(cut[-1] + n)
    slot_sets = [slots[cut[i] : cut[i + 1]] for i in range(6)]

    wvp[...] = jnp.zeros_like(wvp)
    wvp[0:140, 0:1120] = wv_in[...]
    wop[...] = jnp.zeros_like(wop)
    wop[0:70, 0:2240] = wo_in[...]
    xh = lax.div(me.x, 2)
    for k in range(6):
        t = 6 * me.p + k
        r, l = lax.rem(t, 9), lax.div(t, 9)
        wv[me.c, xh, me.z, me.y, me.xl, k // 2, k % 2] = wvp[
            pl.ds(pl.multiple_of(r * 16, 16), 16),
            pl.ds(pl.multiple_of((5 * me.c + l) * 128, 128), 128),
        ]
        r, l = lax.rem(t, 5), lax.div(t, 5)
        wo[me.c, xh, me.z, me.y, me.xl, k // 2, k % 2] = wop[
            pl.ds(pl.multiple_of(r * 16, 16), 16),
            pl.ds(pl.multiple_of((9 * me.c + l) * 128, 128), 128),
        ]

    peers = [me.peer("x", k) for k in (1, 2, 3)] + [me.peer("y", k) for k in (1, 2, 3)]
    peers += [me.peer("z", 1), me.peer("z", -1), me.sibling()]
    peers += [me.row_peer(dy, 1) for dy in (1, 2, 3)]
    barrier = pltpu.get_barrier_semaphore()
    for dev in peers:
        pl.semaphore_signal(barrier, inc=1, device_id=dev, device_id_type=MESH)
    pl.semaphore_wait(barrier, len(peers))

    ga = [gather(wire, me, wv, o) for o in range(3)]
    gb = [gather(wire, me, wo, o) for o in range(3)]
    step(ga)

    tokp[...] = jnp.zeros_like(tokp)
    for i in range(16):
        tokp[:, 144 * i : 144 * i + 140] = tok[:, 140 * i : 140 * i + 140]
    step(ga)
    qp[...] = jnp.zeros_like(qp)
    qp[:, 0:1120] = q_in[...]
    kp[...] = jnp.zeros_like(kp)
    kp[:, 0:1120] = k_in[...]
    step(ga)
    step(gb)
    cotp[me.c] = jnp.zeros((128, 2304), BF)
    cotp[me.c, :, 0:2240] = cot[...]
    ex_cot = wire.send(cotp.at[me.c], cotp.at[me.c], me.sibling())
    for i in range(9):
        tok_t[me.c, 256 * i : 256 * i + 256] = tokp[:, 256 * i : 256 * i + 256].T
    ex_tok = wire.send(tok_t.at[me.c], tok_t.at[me.c], me.sibling())
    part1[...] = jnp.zeros_like(part1)
    part2[...] = jnp.zeros_like(part2)
    att_p[...] = jnp.zeros_like(att_p)
    gvp[me.c] = jnp.zeros((128, 1280), BF)
    rsv_t = rs_v.reshape(16, 48, 16, 128)
    rso_t = rs_o.reshape(16, 48, 16, 128)
    rsv_t[:, 45:48] = jnp.zeros((16, 3, 16, 128), BF)
    rso_t[:, 45:48] = jnp.zeros((16, 3, 16, 128), BF)
    while ga:
        step(ga)
        step(gb)

    wv_t = wv.reshape(2, 16, 48, 16, 128)
    wo_t = wo.reshape(2, 16, 48, 16, 128)
    row = lax.broadcasted_iota(jnp.int32, (128, 128), 0) // 32
    col = lax.broadcasted_iota(jnp.int32, (128, 128), 1) // 32
    heads = (row == col).astype(F32)
    heads_b = heads.astype(BF)

    for group in ((0, 1), (2, 3), (4,), (5, 6), (7, 8)):
        acc = None
        for h in range(2):
            slab = jnp.concatenate(
                [
                    wv_t[s // 5, 8 * h : 8 * h + 8, 9 * (s % 5) : 9 * (s % 5) + 9].reshape(1152, 128)
                    for s in group
                ],
                axis=1,
            )
            part = dot(tokp[:, 1152 * h : 1152 * h + 1152], slab)
            acc = part if acc is None else acc + part
        val[:, 128 * group[0] : 128 * (group[-1] + 1)] = acc.astype(BF)

    def lanes_of(g):
        return pl.ds(pl.multiple_of(g * 128, 128), 128)

    def put(ref, img, g, m, line):
        ref[img, pl.ds(5 * g, 4)] = fold(m * heads).reshape(4, 8, 128)
        ref[img, 5 * g + 4] = jnp.broadcast_to(line, (8, 128))

    def take(ref, img, g):
        m = ref[img, pl.ds(5 * g, 4)].reshape(32, 128)
        m = jnp.concatenate([m, m, m, m], axis=0) * heads
        return m, ref[img, 5 * g + 4][0:1]

    for img in range(2):
        rows = slice(64 * img, 64 * img + 64)

        def state(g, carry, img=img, rows=rows):
            ln = lanes_of(g)
            kf = jnp.maximum(kp[rows, ln], 0)
            line = jnp.sum(kf.astype(F32), axis=0, keepdims=True)
            put(part1, img, g, t_dot(kf, val[rows, ln]), line)
            return carry

        lax.fori_loop(0, 9, state, 0)

    s1 = [seq_sum(wire, me, part1, sib1, row1, tot1)]
    while s1:
        step(s1)
        step(gb)

    for img in range(2):
        rows = slice(64 * img, 64 * img + 64)

        def attend(g, carry, img=img, rows=rows):
            ln = lanes_of(g)
            qf = jnp.maximum(qp[rows, ln], 0)
            kv, kt = take(tot1, img, g)
            hi, lo = split(kv)
            numer = dot(qf, hi) + dot(qf, lo)
            hi, lo = split(qf.astype(F32) * kt)
            denom = dot(hi, heads_b) + dot(lo, heads_b) + 1.0
            ratio = numer / denom
            denf[rows, ln] = denom
            attf[rows, ln] = ratio
            att_h[rows, ln] = ratio.astype(BF)
            return carry

        lax.fori_loop(0, 9, attend, 0)
    for i in range(16):
        att_p[:, 80 * i : 80 * i + 70] = att_h[:, 70 * i : 70 * i + 70]
    for i in range(5):
        att_t[me.c, 256 * i : 256 * i + 256] = att_p[:, 256 * i : 256 * i + 256].T
    ex_att = wire.send(att_t.at[me.c], att_t.at[me.c], me.sibling())

    while gb:
        step(gb)

    def out_rows(i, n):
        return jnp.concatenate(
            [
                wo_t[s // 9, i : i + n, 5 * (s % 9) : 5 * (s % 9) + 5].reshape(80 * n, 128)
                for s in range(18)
            ],
            axis=1,
        )

    ghp[...] = jnp.zeros_like(ghp)
    for i in range(4):
        gh = dot_t(cotp[me.c], out_rows(4 * i, 4))
        for j in range(4):
            at = 70 * (4 * i + j)
            ghp[:, at : at + 70] = gh[:, 80 * j : 80 * j + 70]

    for img in range(2):
        rows = slice(64 * img, 64 * img + 64)

        def grads(g, carry, img=img, rows=rows):
            ln = lanes_of(g)
            q = qp[rows, ln]
            qf = jnp.maximum(q, 0)
            kv, kt = take(tot1, img, g)
            kv_hi, kv_lo = split(kv)
            gn = ghp[rows, ln] / denf[rows, ln]
            hi, lo = split(gn * attf[rows, ln])
            gd = -(dot(hi, heads_b) + dot(lo, heads_b))
            hi, lo = split(gn)
            part = dot_t(hi, kv_hi) + dot_t(lo, kv_hi) + dot_t(hi, kv_lo) + gd * kt
            gqp[rows, ln] = jnp.where(q > 0, part, 0.0).astype(BF)
            line = jnp.sum(qf.astype(F32) * gd, axis=0, keepdims=True)
            put(part2, img, g, t_dot(qf, hi) + t_dot(qf, lo), line)
            return carry

        lax.fori_loop(0, 9, grads, 0)

    s2 = [seq_sum(wire, me, part2, sib2, row2, tot2)]
    step(s2)
    gq_o[...] = gqp[:, 0:1120]
    ex_cot.wait_recv()
    ex_att.wait_recv()
    step(s2)

    cot_half = pl.ds(pl.multiple_of(me.c * 1152, 128), 1152)

    def out_term(i, carry):
        a = jnp.concatenate([att_t[s, pl.ds(pl.multiple_of(160 * i, 32), 160)] for s in (0, 1)], axis=1)
        b = jnp.concatenate([cotp[0, :, cot_half], cotp[1, :, cot_half]], axis=0)
        m = dot(a, b).astype(BF)
        for l in range(9):
            rso_t[pl.ds(2 * i, 2), 5 * l : 5 * l + 5] = m[:, 128 * l : 128 * l + 128].reshape(2, 5, 16, 128)
        return carry

    lax.fori_loop(0, 8, out_term, 0)
    step(s2)
    so = [scatter(wire, me, rs_o, o, slot_sets[o], fin_o) for o in range(3)]
    step(so)
    for i in range(9):
        slab = jnp.concatenate(
            [
                wo_t[s // 9, :, 5 * (s % 9) : 5 * (s % 9) + 5].reshape(1280, 128)
                for s in (2 * i, 2 * i + 1)
            ],
            axis=1,
        )
        width = min(256, 2240 - 256 * i)
        out_o[:, 256 * i : 256 * i + width] = dot(att_p[...], slab).astype(BF)[:, 0:width]
    while s2:
        step(s2)

    for img in range(2):
        rows = slice(64 * img, 64 * img + 64)

        def last_grads(g, carry, img=img, rows=rows):
            ln = lanes_of(g)
            k = kp[rows, ln]
            kf = jnp.maximum(k, 0)
            gs, gt = take(tot2, img, g)
            hi, lo = split(gs)
            gvp[me.c, rows, ln] = (dot(kf, hi) + dot(kf, lo)).astype(BF)
            v = val[rows, ln]
            part = dot_t(v, hi) + dot_t(v, lo) + gt
            gkp[rows, ln] = jnp.where(k > 0, part, 0.0).astype(BF)
            return carry

        lax.fori_loop(0, 9, last_grads, 0)
    ex_gv = wire.send(gvp.at[me.c], gvp.at[me.c], me.sibling())
    step(so)
    gk_o[...] = gkp[:, 0:1120]
    ex_tok.wait_recv()
    ex_gv.wait_recv()

    gv_half = pl.ds(pl.multiple_of(me.c * 640, 128), 640)

    def value_term(i, carry):
        a = jnp.concatenate([tok_t[s, pl.ds(pl.multiple_of(288 * i, 32), 288)] for s in (0, 1)], axis=1)
        b = jnp.concatenate([gvp[0, :, gv_half], gvp[1, :, gv_half]], axis=0)
        m = dot(a, b).astype(BF)
        for l in range(5):
            rsv_t[pl.ds(2 * i, 2), 9 * l : 9 * l + 9] = m[:, 128 * l : 128 * l + 128].reshape(2, 9, 16, 128)
        return carry

    lax.fori_loop(0, 8, value_term, 0)
    sv = [scatter(wire, me, rs_v, o, slot_sets[3 + o], fin_v) for o in range(3)]
    step(sv)
    step(so)

    for i in range(4):
        w = jnp.concatenate(
            [
                wv_t[s // 5, 4 * i : 4 * i + 4, 9 * (s % 5) : 9 * (s % 5) + 9].reshape(576, 128)
                for s in range(9)
            ],
            axis=1,
        )
        gt = dot_t(gvp[me.c, :, 0:1152], w).astype(BF)
        for j in range(4):
            at = 140 * (4 * i + j)
            gtok_o[:, at : at + 140] = gt[:, 144 * j : 144 * j + 140]
        step(so)
    while sv:
        step(so)
        step(sv)
    while so:
        step(so)

    ends = [spread(wire, me, fin_o), spread(wire, me, fin_v)]
    while ends:
        step(ends)
    seq = me.p * 2 + me.c
    fin_vt = fin_v.reshape(2, 48, 16, 128)
    fin_ot = fin_o.reshape(2, 48, 16, 128)

    def slab_of(ref, s, per_core, height):
        tiles = ref[lax.div(s, per_core), pl.ds(lax.rem(s, per_core) * height, height)]
        return tiles.reshape(height * 16, 128)

    first = lax.div(70 * seq, 128)
    shift = 70 * seq - 128 * first
    m = jnp.concatenate([slab_of(fin_vt, jnp.minimum(first + j, 8), 5, 9) for j in range(2)], axis=1)
    gwv_o[...] = pltpu.roll(m, lax.rem(256 - shift, 256), 1)[0:140, 0:70]
    first = lax.div(140 * seq, 128)
    shift = 140 * seq - 128 * first
    m = jnp.concatenate([slab_of(fin_ot, jnp.minimum(first + j, 17), 9, 5) for j in range(3)], axis=1)
    gwo_o[...] = pltpu.roll(m, lax.rem(384 - shift, 384), 1)[0:70, 0:140]
    wire.drain()


def body(tokens, q_raw, k_raw, w_value, w_out, cotangent):
    shape = jax.ShapeDtypeStruct
    weight = VM((2, 2, 8, 4, 2, 3, 2, 16, 128), BF)
    partial = VM((2, 8, 4, 2, 3, 2, 16, 128), BF)
    state = VM((2, 48, 8, 128), F32)
    final = VM((2, 8, 3, 2, 16, 128), F32)
    slots = [s for _ in range(2) for o in range(3) for s in scatter_slots(o)]
    outs = pl.pallas_call(
        kernel,
        out_shape=(
            shape((128, 2240), BF),
            shape((128, 2240), BF),
            shape((128, 1120), BF),
            shape((128, 1120), BF),
            shape((140, 70), F32),
            shape((70, 140), F32),
        ),
        in_specs=[pl.BlockSpec(memory_space=VM)] * 6,
        out_specs=(pl.BlockSpec(memory_space=VM),) * 6,
        scratch_shapes=[
            pltpu.SemaphoreType.DMA((2, N_SEMS)),
            weight,
            weight,
            VM((144, 1408), BF),
            VM((80, 2432), BF),
            VM((128, 2304), BF),
            VM((2, 2304, 128), BF),
            VM((2, 128, 2304), BF),
            VM((128, 1152), BF),
            VM((128, 1152), BF),
            VM((128, 1152), BF),
            VM((128, 1152), F32),
            VM((128, 1152), F32),
            VM((128, 1152), BF),
            VM((128, 1280), BF),
            VM((2, 1280, 128), BF),
            VM((128, 1152), F32),
            VM((2, 128, 1280), BF),
            VM((128, 1152), BF),
            VM((128, 1152), BF),
            state,
            state,
            VM((48, 8, 128), F32),
            VM((48, 8, 128), F32),
            VM((7, 6, 8, 128), F32),
            VM((7, 6, 8, 128), F32),
            state,
            state,
            partial,
            partial,
            final,
            final,
            *slots,
        ],
        compiler_params=pltpu.CompilerParams(
            collective_id=0, has_side_effects=True, vmem_limit_bytes=60 * 2**20
        ),
    )(
        tokens.reshape(128, 2240),
        q_raw.reshape(128, 1120),
        k_raw.reshape(128, 1120),
        w_value,
        w_out,
        cotangent.reshape(128, 2240),
    )
    return (
        outs[0].reshape(2, 64, 2240),
        outs[1].reshape(2, 64, 2240),
        outs[2].reshape(2, 64, 1120),
        outs[3].reshape(2, 64, 1120),
        outs[4],
        outs[5],
    )


def solution(mesh):
    rows = P("dp", "seq", None)
    return jax.shard_map(
        body,
        mesh=mesh,
        in_specs=(rows, rows, rows, P("dp", None), P("dp", None), rows),
        out_specs=(rows, rows, rows, rows, P("dp", "seq"), P("dp", "seq")),
        check_vma=False,
    )
```

```python
import jax
import jax.numpy as jnp
from jax import lax
from jax.experimental import pallas as pl
from jax.experimental.pallas import tpu as pltpu
from jax.sharding import PartitionSpec as P

BF = jnp.bfloat16
F32 = jnp.float32
MESH = pl.DeviceIdType.MESH
VM = pltpu.VMEM
SIZE = {"x": 4, "y": 4, "z": 8}
SCATTER = (("z", "x", "y"), ("x", "y", "z"), ("y", "x", "z"))
PAIRS = ((0, 1), (1, 0), (1, 1), (2, 0), (2, 1), (3, 0), (3, 1))
N_SEMS = 320


class Place:
    def __init__(self):
        dp = lax.axis_index("dp")
        seq = lax.axis_index("seq")
        self.z = lax.rem(dp, 8)
        self.y = lax.div(seq, 4)
        self.xl = lax.rem(lax.div(seq, 2), 2)
        self.c = lax.rem(seq, 2)
        self.xh = lax.div(dp, 8)
        self.x = self.xh * 2 + self.xl
        self.p = self.y * 2 + self.xl

    def step(self, d, k):
        return lax.rem(getattr(self, d) + (k % SIZE[d]), SIZE[d])

    def dev(self, x=None, y=None, z=None, c=None):
        x = self.x if x is None else x
        y = self.y if y is None else y
        z = self.z if z is None else z
        c = self.c if c is None else c
        return (lax.div(x, 2) * 8 + z, (y * 2 + lax.rem(x, 2)) * 2 + c)

    def peer(self, d, k):
        return self.dev(**{d: self.step(d, k)})

    def sibling(self):
        return self.dev(c=1 - self.c)

    def row_peer(self, dy, dx):
        xl = lax.rem(self.xl + dx, 2)
        return self.dev(y=self.step("y", dy), x=self.x - self.xl + xl)

    def index(self, o, open_, d, b, half=None):
        co = {"x": self.x, "y": self.y, "z": self.z}
        for e in open_:
            co[e] = None
        co[d] = b
        every = slice(None)
        x = co["x"]
        xh, xl = (every, every) if x is None else (lax.div(x, 2), lax.rem(x, 2))
        z = every if co["z"] is None else co["z"]
        y = every if co["y"] is None else co["y"]
        out = (xh, z, y, xl, o)
        return out if half is None else out + (half,)


class Wire:
    def __init__(self, sems):
        self.sems = sems
        self.started = []

    def send(self, src, dst, dev):
        k = len(self.started)
        cp = pltpu.make_async_remote_copy(
            src_ref=src,
            dst_ref=dst,
            send_sem=self.sems.at[0, k],
            recv_sem=self.sems.at[1, k],
            device_id=dev,
            device_id_type=MESH,
        )
        cp.start()
        self.started.append(cp)
        return cp

    def drain(self):
        for cp in self.started:
            cp.wait_send()


def gather(wire, me, buf, o, tile=None):
    sib = []

    def share(ref):
        sib.append(wire.send(ref, ref, me.sibling()))

    def piece(xh=None, z=None, y=None, xl=None, half=None):
        every = slice(None)
        i = (me.c,) + tuple(every if v is None else v for v in (xh, z, y, xl)) + (o,)
        return buf.at[i if half is None else i + (half,)]

    def direct(d, ref):
        cps = [wire.send(ref, ref, me.peer(d, k)) for k in range(1, SIZE[d])]
        yield
        for cp in cps:
            cp.wait_recv()

    def ring(d, block):
        share(block(getattr(me, d)))
        steps = SIZE[d] // 2
        for s in range(1, steps + 1):
            hp, hm = (0, 1) if s == steps else (None, None)
            fp = block(me.step(d, -(s - 1)), hp)
            fm = block(me.step(d, s - 1), hm)
            plus = wire.send(fp, fp, me.peer(d, 1))
            minus = wire.send(fm, fm, me.peer(d, -1))
            yield
            plus.wait_recv()
            minus.wait_recv()
            share(block(me.step(d, -s), hp))
            share(block(me.step(d, s), hm))

    if o == 0:
        ref = piece(xh=me.xh, z=me.z, half=tile)
        cp = wire.send(ref, ref, me.dev(x=3 - me.x))
        yield
        cp.wait_recv()
        share(piece(z=me.z, half=tile))
        for s in range(1, 5):
            cps = []
            for sign in (1, -1) if s < 4 else ((1, -1)[tile],):
                ref = piece(z=me.step("z", -sign * (s - 1)), half=tile)
                cps.append((sign, wire.send(ref, ref, me.peer("z", sign))))
            yield
            for sign, cp in cps:
                cp.wait_recv()
                share(piece(z=me.step("z", -sign * s), half=tile))
    elif o == 1:
        yield from direct("z", piece(me.xh, me.z, me.y, me.xl))
        yield from direct("y", piece(xh=me.xh, y=me.y, xl=me.xl))
        yield from ring(
            "x", lambda b, h=None: piece(xh=lax.div(b, 2), xl=lax.rem(b, 2), half=h)
        )
    else:
        yield from direct("z", piece(me.xh, me.z, me.y, me.xl))
        yield from direct("x", piece(xh=me.xh, y=me.y, xl=me.xl))
        yield from ring("y", lambda b, h=None: piece(y=b, half=h))
    yield
    for cp in sib:
        cp.wait_recv()


def scatter(wire, me, buf, o, rx, fin):
    rx = iter(rx)
    dims = SCATTER[o]
    for n, d in enumerate(dims):
        open_ = dims[n + 1 :]
        last = n == 2

        def at(k, half=None):
            return me.index(o, open_, d, me.step(d, k), half)

        own = at(0)
        if d != "z" or n:
            slots = [next(rx) for _ in range(1, SIZE[d])]
            cps = [
                wire.send(buf.at[at(k)], slots[k - 1], me.peer(d, k))
                for k in range(1, SIZE[d])
            ]
            yield
            acc = buf[own].astype(F32)
            for cp, slot in zip(cps, slots):
                cp.wait_recv()
                acc = acc + slot[...].astype(F32)
        else:
            up = [next(rx) for _ in range(4)]
            down = [next(rx) for _ in range(4)]
            for s in range(1, 5):
                k = 5 - s
                hp, hm = (0, 1) if s == 1 else (None, None)
                if s > 1:
                    plus.wait_recv()
                    minus.wait_recv()
                    for sign, slot, half in ((1, up[s - 2], 0), (-1, down[s - 2], 1)):
                        i = at(sign * k, half if s == 2 else None)
                        buf[i] = (buf[i].astype(F32) + slot[...].astype(F32)).astype(BF)
                plus = wire.send(buf.at[at(k, hp)], up[s - 1], me.peer(d, 1))
                minus = wire.send(buf.at[at(-k, hm)], down[s - 1], me.peer(d, -1))
                yield
            plus.wait_recv()
            minus.wait_recv()
            acc = buf[own].astype(F32) + up[3][...].astype(F32) + down[3][...].astype(F32)
        if last:
            fin[me.c, me.p, o] = acc
        else:
            buf[own] = acc.astype(BF)


def scatter_slots(o):
    dims = SCATTER[o]
    out = []
    for n, d in enumerate(dims):
        open_ = dims[n + 1 :]
        shape = ()
        if "x" in open_:
            shape += (2,)
        if "z" in open_:
            shape += (8,)
        if "y" in open_:
            shape += (4,)
        if "x" in open_:
            shape += (2,)
        tile = (16, 128)
        if d != "z" or n:
            out += [VM(shape + (2,) + tile, BF)] * (SIZE[d] - 1)
        else:
            out += ([VM(shape + tile, BF)] + [VM(shape + (2,) + tile, BF)] * 3) * 2
    return out


def spread(wire, me, fin):
    mine = fin.at[me.c, me.p]
    cps = [wire.send(mine, mine, me.row_peer(dy, dx)) for dy, dx in PAIRS]
    yield
    for cp in cps:
        cp.wait_recv()
    half = fin.at[me.c]
    cp = wire.send(half, half, me.sibling())
    yield
    cp.wait_recv()


def seq_sum(wire, me, part, from_sib, from_row, total):
    cp = wire.send(part.at[1 - me.c], from_sib, me.sibling())
    yield
    cp.wait_recv()
    part[me.c] = part[me.c] + from_sib[...]
    cps = []
    for n, (dy, dx) in enumerate(PAIRS):
        p = me.step("y", dy) * 2 + lax.rem(me.xl + dx, 2)
        cps.append(
            wire.send(part.at[me.c, pl.ds(6 * p, 6)], from_row.at[n], me.row_peer(dy, dx))
        )
    yield
    acc = part[me.c, pl.ds(6 * me.p, 6)]
    for n, cp in enumerate(cps):
        cp.wait_recv()
        acc = acc + from_row[n]
    total[me.c, pl.ds(6 * me.p, 6)] = acc
    mine = total.at[me.c, pl.ds(6 * me.p, 6)]
    cps = [wire.send(mine, mine, me.row_peer(dy, dx)) for dy, dx in PAIRS]
    yield
    for cp in cps:
        cp.wait_recv()
    half = total.at[me.c]
    cp = wire.send(half, half, me.sibling())
    yield
    cp.wait_recv()


def step(gens):
    for g in list(gens):
        try:
            next(g)
        except StopIteration:
            gens.remove(g)


def split(a):
    hi = a.astype(BF)
    return hi, (a - hi.astype(F32)).astype(BF)


def dot(a, b):
    return jnp.dot(a, b, preferred_element_type=F32)


def dot_t(a, b):
    return lax.dot_general(a, b, (((1,), (1,)), ((), ())), preferred_element_type=F32)


def t_dot(a, b):
    return lax.dot_general(a, b, (((0,), (0,)), ((), ())), preferred_element_type=F32)


def fold(m):
    return m[0:32] + m[32:64] + m[64:96] + m[96:128]


def kernel(
    tok, q_in, k_in, wv_in, wo_in, cot,
    out_o, gtok_o, gq_o, gk_o, gwv_o, gwo_o,
    sems, wv, wo, wvp, wop, tokp, tok_t, cotp, qp, kp, val, attf, denf, att_h, att_p, att_t,
    ghp, gvp, gqp, gkp, part1, part2, sib1, sib2, row1, row2, tot1, tot2,
    rs_v, rs_o, fin_v, fin_o, *slots,
):
    me = Place()
    wire = Wire(sems)
    per = [len(scatter_slots(o)) for o in range(3)]
    cut = [0]
    for n in per * 2:
        cut.append(cut[-1] + n)
    slot_sets = [slots[cut[i] : cut[i + 1]] for i in range(6)]

    wv_t = wv.reshape(2, 16, 48, 16, 128)
    wo_t = wo.reshape(2, 16, 48, 16, 128)
    shard = me.xh * 8 + me.z
    wvp[...] = jnp.zeros_like(wvp)
    wvp[0:140, 0:1120] = wv_in[...]
    for l in range(5):
        slab = wvp[:, pl.ds(pl.multiple_of((5 * me.c + l) * 128, 128), 128)]
        wv_t[me.c, shard, 9 * l : 9 * l + 9] = slab.reshape(9, 16, 128)
    wv_t[me.c, shard, 45:48] = jnp.zeros((3, 16, 128), BF)
    wop[...] = jnp.zeros_like(wop)
    wop[0:70, 0:2240] = wo_in[...]
    for l in range(9):
        slab = wop[:, pl.ds(pl.multiple_of((9 * me.c + l) * 128, 128), 128)]
        wo_t[me.c, shard, 5 * l : 5 * l + 5] = slab.reshape(5, 16, 128)
    wo_t[me.c, shard, 45:48] = jnp.zeros((3, 16, 128), BF)

    peers = [me.peer("x", k) for k in (1, 2, 3)] + [me.peer("y", k) for k in (1, 2, 3)]
    peers += [me.peer("z", k) for k in range(1, 8)] + [me.sibling()]
    peers += [me.row_peer(dy, 1) for dy in (1, 2, 3)]
    barrier = pltpu.get_barrier_semaphore()
    for dev in peers:
        pl.semaphore_signal(barrier, inc=1, device_id=dev, device_id_type=MESH)
    pl.semaphore_wait(barrier, len(peers))

    a0 = [gather(wire, me, wv, 0, t) for t in range(2)]
    b0 = [gather(wire, me, wo, 0, t) for t in range(2)]
    a1, a2, b1, b2 = [[gather(wire, me, w, o)] for w in (wv, wo) for o in (1, 2)]

    def go(*order):
        for g in order:
            step(g)

    go(a1, a2, a0)
    go(b1, b2, a0)

    tokp[...] = jnp.zeros_like(tokp)
    for i in range(16):
        tokp[:, 144 * i : 144 * i + 140] = tok[:, 140 * i : 140 * i + 140]
    go(a1, a2, b1, b2, a0)
    qp[...] = jnp.zeros_like(qp)
    qp[:, 0:1120] = q_in[...]
    kp[...] = jnp.zeros_like(kp)
    kp[:, 0:1120] = k_in[...]
    part1[...] = jnp.zeros_like(part1)
    part2[...] = jnp.zeros_like(part2)
    go(a1, a2, a0, b0)
    att_p[...] = jnp.zeros_like(att_p)
    gvp[me.c] = jnp.zeros((128, 1280), BF)
    cotp[me.c] = jnp.zeros((128, 2304), BF)
    cotp[me.c, :, 0:2240] = cot[...]
    go(a0)
    for i in range(9):
        tok_t[me.c, 256 * i : 256 * i + 256] = tokp[:, 256 * i : 256 * i + 256].T
    rsv_t = rs_v.reshape(16, 48, 16, 128)
    rso_t = rs_o.reshape(16, 48, 16, 128)
    rsv_t[:, 45:48] = jnp.zeros((16, 3, 16, 128), BF)
    rso_t[:, 45:48] = jnp.zeros((16, 3, 16, 128), BF)
    ghp[...] = jnp.zeros_like(ghp)
    go(a1, a2, a0, b0, b1, b2, a1, a2)
    go(a0, a1, a2)
    ex_cot = wire.send(cotp.at[me.c], cotp.at[me.c], me.sibling())
    ex_tok = wire.send(tok_t.at[me.c], tok_t.at[me.c], me.sibling())

    row = lax.broadcasted_iota(jnp.int32, (128, 128), 0) // 32
    col = lax.broadcasted_iota(jnp.int32, (128, 128), 1) // 32
    heads = (row == col).astype(F32)
    heads_b = heads.astype(BF)

    for group in ((0, 1), (2, 3), (4,), (5, 6), (7, 8)):
        acc = None
        for h in range(2):
            slab = jnp.concatenate(
                [
                    wv_t[s // 5, 8 * h : 8 * h + 8, 9 * (s % 5) : 9 * (s % 5) + 9].reshape(1152, 128)
                    for s in group
                ],
                axis=1,
            )
            part = dot(tokp[:, 1152 * h : 1152 * h + 1152], slab)
            acc = part if acc is None else acc + part
        val[:, 128 * group[0] : 128 * (group[-1] + 1)] = acc.astype(BF)
        if group[0] == 2:
            step(b0)

    def lanes_of(g):
        return pl.ds(pl.multiple_of(g * 128, 128), 128)

    def put(ref, img, g, m, line):
        ref[img, pl.ds(5 * g, 4)] = fold(m * heads).reshape(4, 8, 128)
        ref[img, 5 * g + 4] = jnp.broadcast_to(line, (8, 128))

    def take(ref, img, g):
        m = ref[img, pl.ds(5 * g, 4)].reshape(32, 128)
        m = jnp.concatenate([m, m, m, m], axis=0) * heads
        return m, ref[img, 5 * g + 4][0:1]

    for img in range(2):
        rows = slice(64 * img, 64 * img + 64)

        def state(g, carry, img=img, rows=rows):
            ln = lanes_of(g)
            kf = jnp.maximum(kp[rows, ln], 0)
            line = jnp.sum(kf.astype(F32), axis=0, keepdims=True)
            put(part1, img, g, t_dot(kf, val[rows, ln]), line)
            return carry

        lax.fori_loop(0, 9, state, 0, unroll=3)

    s1 = [seq_sum(wire, me, part1, sib1, row1, tot1)]
    go(s1, b0, s1, s1, b1, b2, b0, s1, s1)

    for img in range(2):
        rows = slice(64 * img, 64 * img + 64)

        def attend(g, carry, img=img, rows=rows):
            ln = lanes_of(g)
            qf = jnp.maximum(qp[rows, ln], 0)
            kv, kt = take(tot1, img, g)
            hi, lo = split(kv)
            numer = dot(qf, hi) + dot(qf, lo)
            hi, lo = split(qf.astype(F32) * kt)
            denom = dot(hi, heads_b) + dot(lo, heads_b) + 1.0
            ratio = numer / denom
            denf[rows, ln] = denom
            attf[rows, ln] = ratio
            att_h[rows, ln] = ratio.astype(BF)
            return carry

        lax.fori_loop(0, 9, attend, 0, unroll=3)
    for i in range(16):
        att_p[:, 80 * i : 80 * i + 70] = att_h[:, 70 * i : 70 * i + 70]
    for i in range(5):
        att_t[me.c, 256 * i : 256 * i + 256] = att_p[:, 256 * i : 256 * i + 256].T
    ex_att = wire.send(att_t.at[me.c], att_t.at[me.c], me.sibling())
    while b0 or b1 or b2:
        step(b1)
        step(b2)
        step(b0)

    ex_cot.wait_recv()
    ex_att.wait_recv()

    cot_half = pl.ds(pl.multiple_of(me.c * 1152, 128), 1152)

    def out_term(i, carry):
        a = jnp.concatenate([att_t[s, pl.ds(pl.multiple_of(160 * i, 32), 160)] for s in (0, 1)], axis=1)
        b = jnp.concatenate([cotp[0, :, cot_half], cotp[1, :, cot_half]], axis=0)
        m = dot(a, b).astype(BF)
        for l in range(9):
            rso_t[pl.ds(2 * i, 2), 5 * l : 5 * l + 5] = m[:, 128 * l : 128 * l + 128].reshape(2, 5, 16, 128)
        return carry

    lax.fori_loop(0, 8, out_term, 0)
    so = [scatter(wire, me, rs_o, o, slot_sets[o], fin_o) for o in range(3)]
    so_ring = so[:1]
    step(so)

    def out_rows(i, n):
        return jnp.concatenate(
            [
                wo_t[s // 9, i : i + n, 5 * (s % 9) : 5 * (s % 9) + 5].reshape(80 * n, 128)
                for s in range(18)
            ],
            axis=1,
        )

    for i in range(4):
        gh = dot_t(cotp[me.c], out_rows(4 * i, 4))
        for j in range(4):
            at = 70 * (4 * i + j)
            ghp[:, at : at + 70] = gh[:, 80 * j : 80 * j + 70]
        if i == 2:
            step(so_ring)

    for img in range(2):
        rows = slice(64 * img, 64 * img + 64)

        def grads(g, carry, img=img, rows=rows):
            ln = lanes_of(g)
            q = qp[rows, ln]
            qf = jnp.maximum(q, 0)
            kv, kt = take(tot1, img, g)
            kv_hi, kv_lo = split(kv)
            gn = ghp[rows, ln] / denf[rows, ln]
            hi, lo = split(gn * attf[rows, ln])
            gd = -(dot(hi, heads_b) + dot(lo, heads_b))
            hi, lo = split(gn)
            part = dot_t(hi, kv_hi) + dot_t(lo, kv_hi) + dot_t(hi, kv_lo) + gd * kt
            gqp[rows, ln] = jnp.where(q > 0, part, 0.0).astype(BF)
            line = jnp.sum(qf.astype(F32) * gd, axis=0, keepdims=True)
            put(part2, img, g, t_dot(qf, hi) + t_dot(qf, lo), line)
            return carry

        lax.fori_loop(0, 9, grads, 0, unroll=3)

    s2 = [seq_sum(wire, me, part2, sib2, row2, tot2)]
    step(s2)
    gq_o[...] = gqp[:, 0:1120]
    step(so_ring)
    step(s2)

    step(so_ring)
    step(s2)
    for i in range(9):
        slab = jnp.concatenate(
            [
                wo_t[s // 9, :, 5 * (s % 9) : 5 * (s % 9) + 5].reshape(1280, 128)
                for s in (2 * i, 2 * i + 1)
            ],
            axis=1,
        )
        width = min(256, 2240 - 256 * i)
        out_o[:, 256 * i : 256 * i + width] = dot(att_p[...], slab).astype(BF)[:, 0:width]
    step(so)
    while s2:
        step(s2)

    for img in range(2):
        rows = slice(64 * img, 64 * img + 64)

        def last_grads(g, carry, img=img, rows=rows):
            ln = lanes_of(g)
            k = kp[rows, ln]
            kf = jnp.maximum(k, 0)
            gs, gt = take(tot2, img, g)
            hi, lo = split(gs)
            gvp[me.c, rows, ln] = (dot(kf, hi) + dot(kf, lo)).astype(BF)
            v = val[rows, ln]
            part = dot_t(v, hi) + dot_t(v, lo) + gt
            gkp[rows, ln] = jnp.where(k > 0, part, 0.0).astype(BF)
            return carry

        lax.fori_loop(0, 9, last_grads, 0, unroll=3)
    ex_gv = wire.send(gvp.at[me.c], gvp.at[me.c], me.sibling())
    step(so)
    gk_o[...] = gkp[:, 0:1120]
    ex_tok.wait_recv()
    ex_gv.wait_recv()

    gv_half = pl.ds(pl.multiple_of(me.c * 640, 128), 640)

    def value_term(i, carry):
        a = jnp.concatenate([tok_t[s, pl.ds(pl.multiple_of(288 * i, 32), 288)] for s in (0, 1)], axis=1)
        b = jnp.concatenate([gvp[0, :, gv_half], gvp[1, :, gv_half]], axis=0)
        m = dot(a, b).astype(BF)
        for l in range(5):
            rsv_t[pl.ds(2 * i, 2), 9 * l : 9 * l + 9] = m[:, 128 * l : 128 * l + 128].reshape(2, 9, 16, 128)
        return carry

    lax.fori_loop(0, 8, value_term, 0)
    sv = [scatter(wire, me, rs_v, o, slot_sets[3 + o], fin_v) for o in range(3)]
    sv_ring = sv[:1]
    step(sv)
    while so:
        step(so)
    eo = [spread(wire, me, fin_o)]
    step(eo)

    for i in range(4):
        w = jnp.concatenate(
            [
                wv_t[s // 5, 4 * i : 4 * i + 4, 9 * (s % 5) : 9 * (s % 5) + 9].reshape(576, 128)
                for s in range(9)
            ],
            axis=1,
        )
        gt = dot_t(gvp[me.c, :, 0:1152], w).astype(BF)
        for j in range(4):
            at = 140 * (4 * i + j)
            gtok_o[:, at : at + 140] = gt[:, 144 * j : 144 * j + 140]
        if i < 3:
            step(sv_ring)
    step(eo)
    while sv:
        step(sv)
    ends = [spread(wire, me, fin_v)] + eo
    while ends:
        step(ends)
    seq = me.p * 2 + me.c
    fin_vt = fin_v.reshape(2, 48, 16, 128)
    fin_ot = fin_o.reshape(2, 48, 16, 128)

    def slab_of(ref, s, per_core, height):
        tiles = ref[lax.div(s, per_core), pl.ds(lax.rem(s, per_core) * height, height)]
        return tiles.reshape(height * 16, 128)

    first = lax.div(70 * seq, 128)
    shift = 70 * seq - 128 * first
    m = jnp.concatenate([slab_of(fin_vt, jnp.minimum(first + j, 8), 5, 9) for j in range(2)], axis=1)
    gwv_o[...] = pltpu.roll(m, lax.rem(256 - shift, 256), 1)[0:140, 0:70]
    first = lax.div(140 * seq, 128)
    shift = 140 * seq - 128 * first
    m = jnp.concatenate([slab_of(fin_ot, jnp.minimum(first + j, 17), 9, 5) for j in range(3)], axis=1)
    gwo_o[...] = pltpu.roll(m, lax.rem(384 - shift, 384), 1)[0:70, 0:140]
    wire.drain()


def hand_over(*refs):
    for i in range(6):
        refs[6 + i][...] = refs[i][...]


def body(tokens, q_raw, k_raw, w_value, w_out, cotangent):
    shape = jax.ShapeDtypeStruct
    weight = VM((2, 2, 8, 4, 2, 3, 2, 16, 128), BF)
    partial = VM((2, 8, 4, 2, 3, 2, 16, 128), BF)
    state = VM((2, 48, 8, 128), F32)
    final = VM((2, 8, 3, 2, 16, 128), F32)
    slots = [s for _ in range(2) for o in range(3) for s in scatter_slots(o)]
    outs = pl.pallas_call(
        kernel,
        out_shape=(
            shape((128, 2240), BF),
            shape((128, 2240), BF),
            shape((128, 1120), BF),
            shape((128, 1120), BF),
            shape((140, 70), F32),
            shape((70, 140), F32),
        ),
        in_specs=[pl.BlockSpec(memory_space=VM)] * 6,
        out_specs=(pl.BlockSpec(memory_space=VM),) * 6,
        scratch_shapes=[
            pltpu.SemaphoreType.DMA((2, N_SEMS)),
            weight,
            weight,
            VM((144, 1408), BF),
            VM((80, 2432), BF),
            VM((128, 2304), BF),
            VM((2, 2304, 128), BF),
            VM((2, 128, 2304), BF),
            VM((128, 1152), BF),
            VM((128, 1152), BF),
            VM((128, 1152), BF),
            VM((128, 1152), F32),
            VM((128, 1152), F32),
            VM((128, 1152), BF),
            VM((128, 1280), BF),
            VM((2, 1280, 128), BF),
            VM((128, 1152), F32),
            VM((2, 128, 1280), BF),
            VM((128, 1152), BF),
            VM((128, 1152), BF),
            state,
            state,
            VM((48, 8, 128), F32),
            VM((48, 8, 128), F32),
            VM((7, 6, 8, 128), F32),
            VM((7, 6, 8, 128), F32),
            state,
            state,
            partial,
            partial,
            final,
            final,
            *slots,
        ],
        compiler_params=pltpu.CompilerParams(
            collective_id=0, has_side_effects=True, vmem_limit_bytes=60 * 2**20
        ),
    )(
        tokens.reshape(128, 2240),
        q_raw.reshape(128, 1120),
        k_raw.reshape(128, 1120),
        w_value,
        w_out,
        cotangent.reshape(128, 2240),
    )
    outs = pl.pallas_call(
        hand_over,
        out_shape=tuple(shape(o.shape, o.dtype) for o in outs),
        in_specs=[pl.BlockSpec(memory_space=VM)] * 6,
        out_specs=(pl.BlockSpec(memory_space=VM),) * 6,
    )(*outs)
    return (
        outs[0].reshape(2, 64, 2240),
        outs[1].reshape(2, 64, 2240),
        outs[2].reshape(2, 64, 1120),
        outs[3].reshape(2, 64, 1120),
        outs[4],
        outs[5],
    )


def solution(mesh):
    rows = P("dp", "seq", None)
    return jax.shard_map(
        body,
        mesh=mesh,
        in_specs=(rows, rows, rows, P("dp", None), P("dp", None), rows),
        out_specs=(rows, rows, rows, rows, P("dp", "seq"), P("dp", "seq")),
        check_vma=False,
    )
```

```python
import jax
import jax.numpy as jnp
from jax import lax
from jax.experimental import pallas as pl
from jax.experimental.pallas import tpu as pltpu
from jax.sharding import PartitionSpec as P

BF = jnp.bfloat16
F32 = jnp.float32
MESH = pl.DeviceIdType.MESH
VM = pltpu.VMEM
SIZE = {"x": 4, "y": 4, "z": 8}
SCATTER = (("z", "x", "y"), ("x", "y", "z"), ("y", "x", "z"))
PAIRS = ((0, 1), (1, 0), (1, 1), (2, 0), (2, 1), (3, 0), (3, 1))
N_SEMS = 320


class Place:
    def __init__(self):
        dp = lax.axis_index("dp")
        seq = lax.axis_index("seq")
        self.z = lax.rem(dp, 8)
        self.y = lax.div(seq, 4)
        self.xl = lax.rem(lax.div(seq, 2), 2)
        self.c = lax.rem(seq, 2)
        self.xh = lax.div(dp, 8)
        self.x = self.xh * 2 + self.xl
        self.p = self.y * 2 + self.xl

    def step(self, d, k):
        return lax.rem(getattr(self, d) + (k % SIZE[d]), SIZE[d])

    def dev(self, x=None, y=None, z=None, c=None):
        x = self.x if x is None else x
        y = self.y if y is None else y
        z = self.z if z is None else z
        c = self.c if c is None else c
        return (lax.div(x, 2) * 8 + z, (y * 2 + lax.rem(x, 2)) * 2 + c)

    def peer(self, d, k):
        return self.dev(**{d: self.step(d, k)})

    def sibling(self):
        return self.dev(c=1 - self.c)

    def row_peer(self, dy, dx, c=None):
        xl = lax.rem(self.xl + dx, 2)
        return self.dev(y=self.step("y", dy), x=self.x - self.xl + xl, c=c)

    def index(self, o, open_, d, b, half=None):
        co = {"x": self.x, "y": self.y, "z": self.z}
        for e in open_:
            co[e] = None
        co[d] = b
        every = slice(None)
        x = co["x"]
        xh, xl = (every, every) if x is None else (lax.div(x, 2), lax.rem(x, 2))
        z = every if co["z"] is None else co["z"]
        y = every if co["y"] is None else co["y"]
        out = (xh, z, y, xl, o)
        return out if half is None else out + (half,)


class Wire:
    def __init__(self, sems):
        self.sems = sems
        self.started = []

    def send(self, src, dst, dev):
        k = len(self.started)
        cp = pltpu.make_async_remote_copy(
            src_ref=src,
            dst_ref=dst,
            send_sem=self.sems.at[0, k],
            recv_sem=self.sems.at[1, k],
            device_id=dev,
            device_id_type=MESH,
        )
        cp.start()
        self.started.append(cp)
        return cp

    def drain(self):
        for cp in self.started:
            cp.wait_send()


def gather(wire, me, buf, o, tile=None):
    sib = []

    def share(ref):
        sib.append(wire.send(ref, ref, me.sibling()))

    def piece(xh=None, z=None, y=None, xl=None, half=None):
        every = slice(None)
        i = (me.c,) + tuple(every if v is None else v for v in (xh, z, y, xl)) + (o,)
        return buf.at[i if half is None else i + (half,)]

    def direct(d, ref):
        cps = [wire.send(ref, ref, me.peer(d, k)) for k in range(1, SIZE[d])]
        yield
        for cp in cps:
            cp.wait_recv()

    def ring(d, block):
        share(block(getattr(me, d)))
        steps = SIZE[d] // 2
        for s in range(1, steps + 1):
            hp, hm = (0, 1) if s == steps else (None, None)
            fp = block(me.step(d, -(s - 1)), hp)
            fm = block(me.step(d, s - 1), hm)
            plus = wire.send(fp, fp, me.peer(d, 1))
            minus = wire.send(fm, fm, me.peer(d, -1))
            yield
            plus.wait_recv()
            minus.wait_recv()
            share(block(me.step(d, -s), hp))
            share(block(me.step(d, s), hm))

    if o == 0:
        ref = piece(xh=me.xh, z=me.z, half=tile)
        cp = wire.send(ref, ref, me.dev(x=3 - me.x))
        yield
        cp.wait_recv()
        share(piece(z=me.z, half=tile))
        for s in range(1, 5):
            cps = []
            for sign in (1, -1) if s < 4 else ((1, -1)[tile],):
                ref = piece(z=me.step("z", -sign * (s - 1)), half=tile)
                cps.append((sign, wire.send(ref, ref, me.peer("z", sign))))
            yield
            for sign, cp in cps:
                cp.wait_recv()
                share(piece(z=me.step("z", -sign * s), half=tile))
    elif o == 1:
        yield from direct("z", piece(me.xh, me.z, me.y, me.xl))
        yield from direct("y", piece(xh=me.xh, y=me.y, xl=me.xl))
        yield from ring(
            "x", lambda b, h=None: piece(xh=lax.div(b, 2), xl=lax.rem(b, 2), half=h)
        )
    else:
        yield from direct("z", piece(me.xh, me.z, me.y, me.xl))
        yield from direct("x", piece(xh=me.xh, y=me.y, xl=me.xl))
        yield from ring("y", lambda b, h=None: piece(y=b, half=h))
    yield
    for cp in sib:
        cp.wait_recv()


def scatter(wire, me, buf, o, rx, fin):
    rx = iter(rx)
    dims = SCATTER[o]
    for n, d in enumerate(dims):
        open_ = dims[n + 1 :]
        last = n == 2

        def at(k, half=None):
            return me.index(o, open_, d, me.step(d, k), half)

        own = at(0)
        if d != "z" or n:
            slots = [next(rx) for _ in range(1, SIZE[d])]
            cps = [
                wire.send(buf.at[at(k)], slots[k - 1], me.peer(d, k))
                for k in range(1, SIZE[d])
            ]
            yield
            acc = buf[own].astype(F32)
            for cp, slot in zip(cps, slots):
                cp.wait_recv()
                acc = acc + slot[...].astype(F32)
        else:
            up = [next(rx) for _ in range(4)]
            down = [next(rx) for _ in range(4)]
            for s in range(1, 5):
                k = 5 - s
                hp, hm = (0, 1) if s == 1 else (None, None)
                if s > 1:
                    plus.wait_recv()
                    minus.wait_recv()
                    for sign, slot, half in ((1, up[s - 2], 0), (-1, down[s - 2], 1)):
                        i = at(sign * k, half if s == 2 else None)
                        buf[i] = (buf[i].astype(F32) + slot[...].astype(F32)).astype(BF)
                plus = wire.send(buf.at[at(k, hp)], up[s - 1], me.peer(d, 1))
                minus = wire.send(buf.at[at(-k, hm)], down[s - 1], me.peer(d, -1))
                yield
            plus.wait_recv()
            minus.wait_recv()
            acc = buf[own].astype(F32) + up[3][...].astype(F32) + down[3][...].astype(F32)
        if last:
            fin[me.c, me.p, o] = acc
        else:
            buf[own] = acc.astype(BF)


def scatter_slots(o):
    dims = SCATTER[o]
    out = []
    for n, d in enumerate(dims):
        open_ = dims[n + 1 :]
        shape = ()
        if "x" in open_:
            shape += (2,)
        if "z" in open_:
            shape += (8,)
        if "y" in open_:
            shape += (4,)
        if "x" in open_:
            shape += (2,)
        tile = (16, 128)
        if d != "z" or n:
            out += [VM(shape + (2,) + tile, BF)] * (SIZE[d] - 1)
        else:
            out += ([VM(shape + tile, BF)] + [VM(shape + (2,) + tile, BF)] * 3) * 2
    return out


def spread(wire, me, fin):
    mine = fin.at[me.c, me.p]
    cps = [wire.send(mine, mine, me.row_peer(dy, dx)) for dy, dx in PAIRS]
    yield
    for cp in cps:
        cp.wait_recv()
    half = fin.at[me.c]
    cp = wire.send(half, half, me.sibling())
    yield
    cp.wait_recv()


def span(c, p, div):
    first = 5 * c + div(2 * p, 3)
    final = 5 * c + div(6 * p + 5, 9)
    return div(128 * first, 70), div(128 * final + 127, 70)


def deliver(wire, me, fin):
    base = N_SEMS - 16
    seq = me.p * 2 + me.c
    mine = fin.at[me.c, me.p]
    first, final = span(me.c, me.p, lax.div)
    ends = []
    for e in range(5):
        to = first + e
        cp = pltpu.make_async_remote_copy(
            src_ref=mine,
            dst_ref=mine,
            send_sem=wire.sems.at[0, base + e],
            recv_sem=wire.sems.at[1, base + me.c * 8 + me.p],
            device_id=(me.xh * 8 + me.z, jnp.minimum(to, 15)),
            device_id_type=MESH,
        )
        used = (to <= final) & (to <= 15) & (to != seq)
        pl.when(used)(cp.start)
        ends.append((used, cp))
    yield
    for c in range(2):
        for p in range(8):
            lo, hi = span(c, p, lambda a, b: a // b)
            if lo > 15:
                continue
            used = (seq >= lo) & (seq <= hi) & (seq != 2 * p + c)
            cp = pltpu.make_async_remote_copy(
                src_ref=fin.at[c, p],
                dst_ref=fin.at[c, p],
                send_sem=wire.sems.at[0, base + 5],
                recv_sem=wire.sems.at[1, base + c * 8 + p],
                device_id=me.sibling(),
                device_id_type=MESH,
            )
            pl.when(used)(cp.wait_recv)
    for used, cp in ends:
        pl.when(used)(cp.wait_send)


def seq_sum(wire, me, part, from_sib, from_row, total):
    cp = wire.send(part.at[1 - me.c], from_sib, me.sibling())
    yield
    cp.wait_recv()
    part[me.c] = part[me.c] + from_sib[...]
    cps = []
    for n, (dy, dx) in enumerate(PAIRS):
        p = me.step("y", dy) * 2 + lax.rem(me.xl + dx, 2)
        cps.append(
            wire.send(part.at[me.c, pl.ds(6 * p, 6)], from_row.at[n], me.row_peer(dy, dx))
        )
    yield
    acc = part[me.c, pl.ds(6 * me.p, 6)]
    for n, cp in enumerate(cps):
        cp.wait_recv()
        acc = acc + from_row[n]
    total[me.c, pl.ds(6 * me.p, 6)] = acc
    mine = total.at[me.c, pl.ds(6 * me.p, 6)]
    cps = [wire.send(mine, mine, me.row_peer(dy, dx)) for dy, dx in PAIRS]
    yield
    for cp in cps:
        cp.wait_recv()
    half = total.at[me.c]
    cp = wire.send(half, half, me.sibling())
    yield
    cp.wait_recv()


def step(gens):
    for g in list(gens):
        try:
            next(g)
        except StopIteration:
            gens.remove(g)


def split(a):
    hi = a.astype(BF)
    return hi, (a - hi.astype(F32)).astype(BF)


def dot(a, b):
    return jnp.dot(a, b, preferred_element_type=F32)


def dot_t(a, b):
    return lax.dot_general(a, b, (((1,), (1,)), ((), ())), preferred_element_type=F32)


def t_dot(a, b):
    return lax.dot_general(a, b, (((0,), (0,)), ((), ())), preferred_element_type=F32)


def fold(m):
    return m[0:32] + m[32:64] + m[64:96] + m[96:128]


def kernel(
    tok_h, q_h, k_h, wv_in, wo_in, cot_h,
    out_h, gtok_h, gq_h, gk_h, gwv_o, gwo_o,
    local, tok, q_in, k_in, cot, out_o, gtok_o, gq_o, gk_o, sems, wv, wo, wvp, wop, tokp, tok_t, cotp, qp, kp, val, attf, denf, att_h, att_p, att_t,
    ghp, gvp, gqp, gkp, part1, part2, sib1, sib2, row1, row2, tot1, tot2,
    rs_v, rs_o, fin_v, fin_o, *slots,
):
    ins = [
        pltpu.make_async_copy(a, b, local.at[i])
        for i, (a, b) in enumerate(((tok_h, tok), (q_h, q_in), (k_h, k_in), (cot_h, cot)))
    ]
    for cp in ins:
        cp.start()
    leaving = []

    def leave(src, dst):
        cp = pltpu.make_async_copy(src, dst, local.at[4 + len(leaving)])
        cp.start()
        leaving.append(cp)

    me = Place()
    wire = Wire(sems)
    per = [len(scatter_slots(o)) for o in range(3)]
    cut = [0]
    for n in per * 2:
        cut.append(cut[-1] + n)
    slot_sets = [slots[cut[i] : cut[i + 1]] for i in range(6)]

    wv_t = wv.reshape(2, 16, 48, 16, 128)
    wo_t = wo.reshape(2, 16, 48, 16, 128)
    shard = me.xh * 8 + me.z
    wvp[...] = jnp.zeros_like(wvp)
    wvp[0:140, 0:1120] = wv_in[...]
    for l in range(5):
        slab = wvp[:, pl.ds(pl.multiple_of((5 * me.c + l) * 128, 128), 128)]
        wv_t[me.c, shard, 9 * l : 9 * l + 9] = slab.reshape(9, 16, 128)
    wv_t[me.c, shard, 45:48] = jnp.zeros((3, 16, 128), BF)
    wop[...] = jnp.zeros_like(wop)
    wop[0:70, 0:2240] = wo_in[...]
    for l in range(9):
        slab = wop[:, pl.ds(pl.multiple_of((9 * me.c + l) * 128, 128), 128)]
        wo_t[me.c, shard, 5 * l : 5 * l + 5] = slab.reshape(5, 16, 128)
    wo_t[me.c, shard, 45:48] = jnp.zeros((3, 16, 128), BF)

    peers = [me.peer("x", k) for k in (1, 2, 3)] + [me.peer("y", k) for k in (1, 2, 3)]
    peers += [me.peer("z", k) for k in range(1, 8)] + [me.sibling()]
    peers += [me.row_peer(dy, 1) for dy in (1, 2, 3)]
    peers += [me.row_peer(dy, dx, 1 - me.c) for dy, dx in PAIRS]
    barrier = pltpu.get_barrier_semaphore()
    for dev in peers:
        pl.semaphore_signal(barrier, inc=1, device_id=dev, device_id_type=MESH)
    pl.semaphore_wait(barrier, len(peers))

    a0 = [gather(wire, me, wv, 0, t) for t in range(2)]
    b0 = [gather(wire, me, wo, 0, t) for t in range(2)]
    a1, a2, b1, b2 = [[gather(wire, me, w, o)] for w in (wv, wo) for o in (1, 2)]

    def go(*order):
        for g in order:
            step(g)

    go(a1, a2, a0)
    go(b1, b2, a0)

    for cp in ins:
        cp.wait()
    tokp[...] = jnp.zeros_like(tokp)
    for i in range(16):
        tokp[:, 144 * i : 144 * i + 140] = tok[:, 140 * i : 140 * i + 140]
    go(a1, a2, b1, b2, a0)
    qp[...] = jnp.zeros_like(qp)
    qp[:, 0:1120] = q_in[...]
    kp[...] = jnp.zeros_like(kp)
    kp[:, 0:1120] = k_in[...]
    part1[...] = jnp.zeros_like(part1)
    part2[...] = jnp.zeros_like(part2)
    go(a1, a2, a0, b0)
    att_p[...] = jnp.zeros_like(att_p)
    gvp[me.c] = jnp.zeros((128, 1280), BF)
    cotp[me.c] = jnp.zeros((128, 2304), BF)
    cotp[me.c, :, 0:2240] = cot[...]
    go(a0)
    for i in range(9):
        tok_t[me.c, 256 * i : 256 * i + 256] = tokp[:, 256 * i : 256 * i + 256].T
    rsv_t = rs_v.reshape(16, 48, 16, 128)
    rso_t = rs_o.reshape(16, 48, 16, 128)
    rsv_t[:, 45:48] = jnp.zeros((16, 3, 16, 128), BF)
    rso_t[:, 45:48] = jnp.zeros((16, 3, 16, 128), BF)
    ghp[...] = jnp.zeros_like(ghp)
    go(a1, a2, a0, b0, b1, b2, a1, a2)
    go(a0, a1, a2)
    ex_cot = wire.send(cotp.at[me.c], cotp.at[me.c], me.sibling())
    ex_tok = wire.send(tok_t.at[me.c], tok_t.at[me.c], me.sibling())

    row = lax.broadcasted_iota(jnp.int32, (128, 128), 0) // 32
    col = lax.broadcasted_iota(jnp.int32, (128, 128), 1) // 32
    heads = (row == col).astype(F32)
    heads_b = heads.astype(BF)

    for group in ((0, 1), (2, 3), (4,), (5, 6), (7, 8)):
        acc = None
        for h in range(2):
            slab = jnp.concatenate(
                [
                    wv_t[s // 5, 8 * h : 8 * h + 8, 9 * (s % 5) : 9 * (s % 5) + 9].reshape(1152, 128)
                    for s in group
                ],
                axis=1,
            )
            part = dot(tokp[:, 1152 * h : 1152 * h + 1152], slab)
            acc = part if acc is None else acc + part
        val[:, 128 * group[0] : 128 * (group[-1] + 1)] = acc.astype(BF)
        if group[0] == 2:
            step(b0)

    def lanes_of(g):
        return pl.ds(pl.multiple_of(g * 128, 128), 128)

    def put(ref, img, g, m, line):
        ref[img, pl.ds(5 * g, 4)] = fold(m * heads).reshape(4, 8, 128)
        ref[img, 5 * g + 4] = jnp.broadcast_to(line, (8, 128))

    def take(ref, img, g):
        m = ref[img, pl.ds(5 * g, 4)].reshape(32, 128)
        m = jnp.concatenate([m, m, m, m], axis=0) * heads
        return m, ref[img, 5 * g + 4][0:1]

    for img in range(2):
        rows = slice(64 * img, 64 * img + 64)

        def state(g, carry, img=img, rows=rows):
            ln = lanes_of(g)
            kf = jnp.maximum(kp[rows, ln], 0)
            line = jnp.sum(kf.astype(F32), axis=0, keepdims=True)
            put(part1, img, g, t_dot(kf, val[rows, ln]), line)
            return carry

        lax.fori_loop(0, 9, state, 0, unroll=3)

    s1 = [seq_sum(wire, me, part1, sib1, row1, tot1)]
    go(s1, b0, s1, s1, b1, b2, b0, s1, s1)

    for img in range(2):
        rows = slice(64 * img, 64 * img + 64)

        def attend(g, carry, img=img, rows=rows):
            ln = lanes_of(g)
            qf = jnp.maximum(qp[rows, ln], 0)
            kv, kt = take(tot1, img, g)
            hi, lo = split(kv)
            numer = dot(qf, hi) + dot(qf, lo)
            hi, lo = split(qf.astype(F32) * kt)
            denom = dot(hi, heads_b) + dot(lo, heads_b) + 1.0
            ratio = numer / denom
            denf[rows, ln] = denom
            attf[rows, ln] = ratio
            att_h[rows, ln] = ratio.astype(BF)
            return carry

        lax.fori_loop(0, 9, attend, 0, unroll=3)
    for i in range(16):
        att_p[:, 80 * i : 80 * i + 70] = att_h[:, 70 * i : 70 * i + 70]
    for i in range(5):
        att_t[me.c, 256 * i : 256 * i + 256] = att_p[:, 256 * i : 256 * i + 256].T
    ex_att = wire.send(att_t.at[me.c], att_t.at[me.c], me.sibling())
    while b0 or b1 or b2:
        step(b1)
        step(b2)
        step(b0)

    ex_cot.wait_recv()
    ex_att.wait_recv()

    cot_half = pl.ds(pl.multiple_of(me.c * 1152, 128), 1152)

    def out_term(i, carry):
        a = jnp.concatenate([att_t[s, pl.ds(pl.multiple_of(160 * i, 32), 160)] for s in (0, 1)], axis=1)
        b = jnp.concatenate([cotp[0, :, cot_half], cotp[1, :, cot_half]], axis=0)
        m = dot(a, b).astype(BF)
        for l in range(9):
            rso_t[pl.ds(2 * i, 2), 5 * l : 5 * l + 5] = m[:, 128 * l : 128 * l + 128].reshape(2, 5, 16, 128)
        return carry

    lax.fori_loop(0, 8, out_term, 0)
    so = [scatter(wire, me, rs_o, o, slot_sets[o], fin_o) for o in range(3)]
    so_ring = so[:1]
    step(so)

    def out_rows(i, n):
        return jnp.concatenate(
            [
                wo_t[s // 9, i : i + n, 5 * (s % 9) : 5 * (s % 9) + 5].reshape(80 * n, 128)
                for s in range(18)
            ],
            axis=1,
        )

    for i in range(4):
        gh = dot_t(cotp[me.c], out_rows(4 * i, 4))
        for j in range(4):
            at = 70 * (4 * i + j)
            ghp[:, at : at + 70] = gh[:, 80 * j : 80 * j + 70]
        if i == 2:
            step(so_ring)

    for img in range(2):
        rows = slice(64 * img, 64 * img + 64)

        def grads(g, carry, img=img, rows=rows):
            ln = lanes_of(g)
            q = qp[rows, ln]
            qf = jnp.maximum(q, 0)
            kv, kt = take(tot1, img, g)
            kv_hi, kv_lo = split(kv)
            gn = ghp[rows, ln] / denf[rows, ln]
            hi, lo = split(gn * attf[rows, ln])
            gd = -(dot(hi, heads_b) + dot(lo, heads_b))
            hi, lo = split(gn)
            part = dot_t(hi, kv_hi) + dot_t(lo, kv_hi) + dot_t(hi, kv_lo) + gd * kt
            gqp[rows, ln] = jnp.where(q > 0, part, 0.0).astype(BF)
            line = jnp.sum(qf.astype(F32) * gd, axis=0, keepdims=True)
            put(part2, img, g, t_dot(qf, hi) + t_dot(qf, lo), line)
            return carry

        lax.fori_loop(0, 9, grads, 0, unroll=3)

    s2 = [seq_sum(wire, me, part2, sib2, row2, tot2)]
    step(s2)
    gq_o[...] = gqp[:, 0:1120]
    leave(gq_o, gq_h)
    step(so_ring)
    step(s2)

    step(so_ring)
    step(s2)
    for i in range(9):
        slab = jnp.concatenate(
            [
                wo_t[s // 9, :, 5 * (s % 9) : 5 * (s % 9) + 5].reshape(1280, 128)
                for s in (2 * i, 2 * i + 1)
            ],
            axis=1,
        )
        width = min(256, 2240 - 256 * i)
        out_o[:, 256 * i : 256 * i + width] = dot(att_p[...], slab).astype(BF)[:, 0:width]
    step(so)
    while s2:
        step(s2)

    for img in range(2):
        rows = slice(64 * img, 64 * img + 64)

        def last_grads(g, carry, img=img, rows=rows):
            ln = lanes_of(g)
            k = kp[rows, ln]
            kf = jnp.maximum(k, 0)
            gs, gt = take(tot2, img, g)
            hi, lo = split(gs)
            gvp[me.c, rows, ln] = (dot(kf, hi) + dot(kf, lo)).astype(BF)
            v = val[rows, ln]
            part = dot_t(v, hi) + dot_t(v, lo) + gt
            gkp[rows, ln] = jnp.where(k > 0, part, 0.0).astype(BF)
            return carry

        lax.fori_loop(0, 9, last_grads, 0, unroll=3)
    ex_gv = wire.send(gvp.at[me.c], gvp.at[me.c], me.sibling())
    step(so)
    gk_o[...] = gkp[:, 0:1120]
    leave(gk_o, gk_h)
    leave(out_o, out_h)
    ex_tok.wait_recv()
    ex_gv.wait_recv()

    gv_half = pl.ds(pl.multiple_of(me.c * 640, 128), 640)

    def value_term(i, carry):
        a = jnp.concatenate([tok_t[s, pl.ds(pl.multiple_of(288 * i, 32), 288)] for s in (0, 1)], axis=1)
        b = jnp.concatenate([gvp[0, :, gv_half], gvp[1, :, gv_half]], axis=0)
        m = dot(a, b).astype(BF)
        for l in range(5):
            rsv_t[pl.ds(2 * i, 2), 9 * l : 9 * l + 9] = m[:, 128 * l : 128 * l + 128].reshape(2, 9, 16, 128)
        return carry

    lax.fori_loop(0, 8, value_term, 0)
    sv = [scatter(wire, me, rs_v, o, slot_sets[3 + o], fin_v) for o in range(3)]
    sv_ring = sv[:1]
    step(sv)
    while so:
        step(so)
    eo = [spread(wire, me, fin_o)]
    step(eo)

    for i in range(4):
        w = jnp.concatenate(
            [
                wv_t[s // 5, 4 * i : 4 * i + 4, 9 * (s % 5) : 9 * (s % 5) + 9].reshape(576, 128)
                for s in range(9)
            ],
            axis=1,
        )
        gt = dot_t(gvp[me.c, :, 0:1152], w).astype(BF)
        for j in range(4):
            at = 140 * (4 * i + j)
            gtok_o[:, at : at + 140] = gt[:, 144 * j : 144 * j + 140]
        if i < 3:
            step(sv_ring)
    step(sv)
    step(eo)
    while sv:
        step(sv)
    leave(gtok_o, gtok_h)
    ends = [deliver(wire, me, fin_v)] + eo
    while ends:
        step(ends)
    seq = me.p * 2 + me.c
    fin_vt = fin_v.reshape(2, 48, 16, 128)
    fin_ot = fin_o.reshape(2, 48, 16, 128)

    def slab_of(ref, s, per_core, height):
        tiles = ref[lax.div(s, per_core), pl.ds(lax.rem(s, per_core) * height, height)]
        return tiles.reshape(height * 16, 128)

    first = lax.div(70 * seq, 128)
    shift = 70 * seq - 128 * first
    m = jnp.concatenate([slab_of(fin_vt, jnp.minimum(first + j, 8), 5, 9) for j in range(2)], axis=1)
    gwv_o[...] = pltpu.roll(m, lax.rem(256 - shift, 256), 1)[0:140, 0:70]
    first = lax.div(140 * seq, 128)
    shift = 140 * seq - 128 * first
    m = jnp.concatenate([slab_of(fin_ot, jnp.minimum(first + j, 17), 9, 5) for j in range(3)], axis=1)
    gwo_o[...] = pltpu.roll(m, lax.rem(384 - shift, 384), 1)[0:70, 0:140]
    wire.drain()
    for cp in leaving:
        cp.wait()


def hand_over(*refs):
    for i in range(6):
        refs[6 + i][...] = refs[i][...]


def body(tokens, q_raw, k_raw, w_value, w_out, cotangent):
    shape = jax.ShapeDtypeStruct
    weight = VM((2, 2, 8, 4, 2, 3, 2, 16, 128), BF)
    partial = VM((2, 8, 4, 2, 3, 2, 16, 128), BF)
    state = VM((2, 48, 8, 128), F32)
    final = VM((2, 8, 3, 2, 16, 128), F32)
    slots = [s for _ in range(2) for o in range(3) for s in scatter_slots(o)]
    outs = pl.pallas_call(
        kernel,
        out_shape=(
            shape((128, 2240), BF),
            shape((128, 2240), BF),
            shape((128, 1120), BF),
            shape((128, 1120), BF),
            shape((140, 70), F32),
            shape((70, 140), F32),
        ),
        in_specs=[pl.BlockSpec(memory_space=m) for m in (pl.ANY, pl.ANY, pl.ANY, VM, VM, pl.ANY)],
        out_specs=tuple(
            pl.BlockSpec(memory_space=m) for m in (pl.ANY, pl.ANY, pl.ANY, pl.ANY, VM, VM)
        ),
        scratch_shapes=[
            pltpu.SemaphoreType.DMA((8,)),
            VM((128, 2240), BF),
            VM((128, 1120), BF),
            VM((128, 1120), BF),
            VM((128, 2240), BF),
            VM((128, 2240), BF),
            VM((128, 2240), BF),
            VM((128, 1120), BF),
            VM((128, 1120), BF),
            pltpu.SemaphoreType.DMA((2, N_SEMS)),
            weight,
            weight,
            VM((144, 1408), BF),
            VM((80, 2432), BF),
            VM((128, 2304), BF),
            VM((2, 2304, 128), BF),
            VM((2, 128, 2304), BF),
            VM((128, 1152), BF),
            VM((128, 1152), BF),
            VM((128, 1152), BF),
            VM((128, 1152), F32),
            VM((128, 1152), F32),
            VM((128, 1152), BF),
            VM((128, 1280), BF),
            VM((2, 1280, 128), BF),
            VM((128, 1152), F32),
            VM((2, 128, 1280), BF),
            VM((128, 1152), BF),
            VM((128, 1152), BF),
            state,
            state,
            VM((48, 8, 128), F32),
            VM((48, 8, 128), F32),
            VM((7, 6, 8, 128), F32),
            VM((7, 6, 8, 128), F32),
            state,
            state,
            partial,
            partial,
            final,
            final,
            *slots,
        ],
        compiler_params=pltpu.CompilerParams(
            collective_id=0, has_side_effects=True, vmem_limit_bytes=60 * 2**20
        ),
    )(
        tokens.reshape(128, 2240),
        q_raw.reshape(128, 1120),
        k_raw.reshape(128, 1120),
        w_value,
        w_out,
        cotangent.reshape(128, 2240),
    )
    outs = pl.pallas_call(
        hand_over,
        out_shape=tuple(shape(o.shape, o.dtype) for o in outs),
        in_specs=[pl.BlockSpec(memory_space=VM)] * 6,
        out_specs=(pl.BlockSpec(memory_space=VM),) * 6,
    )(*outs)
    return (
        outs[0].reshape(2, 64, 2240),
        outs[1].reshape(2, 64, 2240),
        outs[2].reshape(2, 64, 1120),
        outs[3].reshape(2, 64, 1120),
        outs[4],
        outs[5],
    )


def solution(mesh):
    rows = P("dp", "seq", None)
    return jax.shard_map(
        body,
        mesh=mesh,
        in_specs=(rows, rows, rows, P("dp", None), P("dp", None), rows),
        out_specs=(rows, rows, rows, rows, P("dp", "seq"), P("dp", "seq")),
        check_vma=False,
    )
```

```python
import jax
import jax.numpy as jnp
from jax import lax
from jax.experimental import pallas as pl
from jax.experimental.pallas import tpu as pltpu
from jax.sharding import PartitionSpec as P

BF = jnp.bfloat16
F32 = jnp.float32
MESH = pl.DeviceIdType.MESH
VM = pltpu.VMEM
SIZE = {"x": 4, "y": 4, "z": 8}
SCATTER = (("z", "x", "y"), ("x", "y", "z"), ("y", "x", "z"))
PAIRS = ((0, 1), (1, 0), (1, 1), (2, 0), (2, 1), (3, 0), (3, 1))
N_SEMS = 320


class Place:
    def __init__(self):
        dp = lax.axis_index("dp")
        seq = lax.axis_index("seq")
        self.z = lax.rem(dp, 8)
        self.y = lax.div(seq, 4)
        self.xl = lax.rem(lax.div(seq, 2), 2)
        self.c = lax.rem(seq, 2)
        self.xh = lax.div(dp, 8)
        self.x = self.xh * 2 + self.xl
        self.p = self.y * 2 + self.xl

    def step(self, d, k):
        return lax.rem(getattr(self, d) + (k % SIZE[d]), SIZE[d])

    def dev(self, x=None, y=None, z=None, c=None):
        x = self.x if x is None else x
        y = self.y if y is None else y
        z = self.z if z is None else z
        c = self.c if c is None else c
        return (lax.div(x, 2) * 8 + z, (y * 2 + lax.rem(x, 2)) * 2 + c)

    def peer(self, d, k):
        return self.dev(**{d: self.step(d, k)})

    def sibling(self):
        return self.dev(c=1 - self.c)

    def row_peer(self, dy, dx, c=None):
        xl = lax.rem(self.xl + dx, 2)
        return self.dev(y=self.step("y", dy), x=self.x - self.xl + xl, c=c)

    def index(self, o, open_, d, b, half=None):
        co = {"x": self.x, "y": self.y, "z": self.z}
        for e in open_:
            co[e] = None
        co[d] = b
        every = slice(None)
        x = co["x"]
        xh, xl = (every, every) if x is None else (lax.div(x, 2), lax.rem(x, 2))
        z = every if co["z"] is None else co["z"]
        y = every if co["y"] is None else co["y"]
        out = (xh, z, y, xl, o)
        return out if half is None else out + (half,)


class Wire:
    def __init__(self, sems):
        self.sems = sems
        self.started = []

    def send(self, src, dst, dev):
        k = len(self.started)
        cp = pltpu.make_async_remote_copy(
            src_ref=src,
            dst_ref=dst,
            send_sem=self.sems.at[0, k],
            recv_sem=self.sems.at[1, k],
            device_id=dev,
            device_id_type=MESH,
        )
        cp.start()
        self.started.append(cp)
        return cp

    def drain(self):
        for cp in self.started:
            cp.wait_send()


def gather(wire, me, buf, o, tile=None):
    sib = []

    def share(ref):
        sib.append(wire.send(ref, ref, me.sibling()))

    def piece(xh=None, z=None, y=None, xl=None, half=None):
        every = slice(None)
        i = (me.c,) + tuple(every if v is None else v for v in (xh, z, y, xl)) + (o,)
        return buf.at[i if half is None else i + (half,)]

    def direct(d, ref):
        cps = [wire.send(ref, ref, me.peer(d, k)) for k in range(1, SIZE[d])]
        yield
        for cp in cps:
            cp.wait_recv()

    def ring(d, block):
        share(block(getattr(me, d)))
        steps = SIZE[d] // 2
        for s in range(1, steps + 1):
            hp, hm = (0, 1) if s == steps else (None, None)
            fp = block(me.step(d, -(s - 1)), hp)
            fm = block(me.step(d, s - 1), hm)
            plus = wire.send(fp, fp, me.peer(d, 1))
            minus = wire.send(fm, fm, me.peer(d, -1))
            yield
            plus.wait_recv()
            minus.wait_recv()
            share(block(me.step(d, -s), hp))
            share(block(me.step(d, s), hm))

    if o == 0:
        ref = piece(xh=me.xh, z=me.z, half=tile)
        cp = wire.send(ref, ref, me.dev(x=3 - me.x))
        yield
        cp.wait_recv()
        share(piece(z=me.z, half=tile))
        for s in range(1, 5):
            cps = []
            for sign in (1, -1) if s < 4 else ((1, -1)[tile],):
                ref = piece(z=me.step("z", -sign * (s - 1)), half=tile)
                cps.append((sign, wire.send(ref, ref, me.peer("z", sign))))
            yield
            for sign, cp in cps:
                cp.wait_recv()
                share(piece(z=me.step("z", -sign * s), half=tile))
    elif o == 1:
        yield from direct("z", piece(me.xh, me.z, me.y, me.xl))
        yield from direct("y", piece(xh=me.xh, y=me.y, xl=me.xl))
        yield from ring(
            "x", lambda b, h=None: piece(xh=lax.div(b, 2), xl=lax.rem(b, 2), half=h)
        )
    else:
        yield from direct("z", piece(me.xh, me.z, me.y, me.xl))
        yield from direct("x", piece(xh=me.xh, y=me.y, xl=me.xl))
        yield from ring("y", lambda b, h=None: piece(y=b, half=h))
    yield
    for cp in sib:
        cp.wait_recv()


def scatter(wire, me, buf, o, rx, fin):
    rx = iter(rx)
    dims = SCATTER[o]
    for n, d in enumerate(dims):
        open_ = dims[n + 1 :]
        last = n == 2

        def at(k, half=None):
            return me.index(o, open_, d, me.step(d, k), half)

        own = at(0)
        if d != "z" or n:
            slots = [next(rx) for _ in range(1, SIZE[d])]
            cps = [
                wire.send(buf.at[at(k)], slots[k - 1], me.peer(d, k))
                for k in range(1, SIZE[d])
            ]
            yield
            acc = buf[own].astype(F32)
            for cp, slot in zip(cps, slots):
                cp.wait_recv()
                acc = acc + slot[...].astype(F32)
        else:
            up = [next(rx) for _ in range(4)]
            down = [next(rx) for _ in range(4)]
            for s in range(1, 5):
                k = 5 - s
                hp, hm = (0, 1) if s == 1 else (None, None)
                if s > 1:
                    plus.wait_recv()
                    minus.wait_recv()
                    for sign, slot, half in ((1, up[s - 2], 0), (-1, down[s - 2], 1)):
                        i = at(sign * k, half if s == 2 else None)
                        buf[i] = (buf[i].astype(F32) + slot[...].astype(F32)).astype(BF)
                plus = wire.send(buf.at[at(k, hp)], up[s - 1], me.peer(d, 1))
                minus = wire.send(buf.at[at(-k, hm)], down[s - 1], me.peer(d, -1))
                yield
            plus.wait_recv()
            minus.wait_recv()
            acc = buf[own].astype(F32) + up[3][...].astype(F32) + down[3][...].astype(F32)
        if last:
            fin[me.c, me.p, o] = acc
        else:
            buf[own] = acc.astype(BF)


def scatter_slots(o):
    dims = SCATTER[o]
    out = []
    for n, d in enumerate(dims):
        open_ = dims[n + 1 :]
        shape = ()
        if "x" in open_:
            shape += (2,)
        if "z" in open_:
            shape += (8,)
        if "y" in open_:
            shape += (4,)
        if "x" in open_:
            shape += (2,)
        tile = (16, 128)
        if d != "z" or n:
            out += [VM(shape + (2,) + tile, BF)] * (SIZE[d] - 1)
        else:
            out += ([VM(shape + tile, BF)] + [VM(shape + (2,) + tile, BF)] * 3) * 2
    return out


def spread(wire, me, fin):
    mine = fin.at[me.c, me.p]
    cps = [wire.send(mine, mine, me.row_peer(dy, dx)) for dy, dx in PAIRS]
    yield
    for cp in cps:
        cp.wait_recv()
    half = fin.at[me.c]
    cp = wire.send(half, half, me.sibling())
    yield
    cp.wait_recv()


def span(c, p, div):
    first = 5 * c + div(2 * p, 3)
    final = 5 * c + div(6 * p + 5, 9)
    return div(128 * first, 70), div(128 * final + 127, 70)


def deliver(wire, me, fin):
    base = N_SEMS - 16
    seq = me.p * 2 + me.c
    mine = fin.at[me.c, me.p]
    first, final = span(me.c, me.p, lax.div)
    ends = []
    for e in range(5):
        to = first + e
        cp = pltpu.make_async_remote_copy(
            src_ref=mine,
            dst_ref=mine,
            send_sem=wire.sems.at[0, base + e],
            recv_sem=wire.sems.at[1, base + me.c * 8 + me.p],
            device_id=(me.xh * 8 + me.z, jnp.minimum(to, 15)),
            device_id_type=MESH,
        )
        used = (to <= final) & (to <= 15) & (to != seq)
        pl.when(used)(cp.start)
        ends.append((used, cp))
    yield
    for c in range(2):
        for p in range(8):
            lo, hi = span(c, p, lambda a, b: a // b)
            if lo > 15:
                continue
            used = (seq >= lo) & (seq <= hi) & (seq != 2 * p + c)
            cp = pltpu.make_async_remote_copy(
                src_ref=fin.at[c, p],
                dst_ref=fin.at[c, p],
                send_sem=wire.sems.at[0, base + 5],
                recv_sem=wire.sems.at[1, base + c * 8 + p],
                device_id=me.sibling(),
                device_id_type=MESH,
            )
            pl.when(used)(cp.wait_recv)
    for used, cp in ends:
        pl.when(used)(cp.wait_send)


def seq_sum(wire, me, part, from_sib, from_row, total):
    cp = wire.send(part.at[1 - me.c], from_sib, me.sibling())
    yield
    cp.wait_recv()
    part[me.c] = part[me.c] + from_sib[...]
    cps = []
    for n, (dy, dx) in enumerate(PAIRS):
        p = me.step("y", dy) * 2 + lax.rem(me.xl + dx, 2)
        cps.append(
            wire.send(part.at[me.c, pl.ds(6 * p, 6)], from_row.at[n], me.row_peer(dy, dx))
        )
    yield
    acc = part[me.c, pl.ds(6 * me.p, 6)]
    for n, cp in enumerate(cps):
        cp.wait_recv()
        acc = acc + from_row[n]
    total[me.c, pl.ds(6 * me.p, 6)] = acc
    mine = total.at[me.c, pl.ds(6 * me.p, 6)]
    cps = [wire.send(mine, mine, me.row_peer(dy, dx)) for dy, dx in PAIRS]
    yield
    for cp in cps:
        cp.wait_recv()
    half = total.at[me.c]
    cp = wire.send(half, half, me.sibling())
    yield
    cp.wait_recv()


def step(gens):
    for g in list(gens):
        try:
            next(g)
        except StopIteration:
            gens.remove(g)


def split(a):
    hi = a.astype(BF)
    return hi, (a - hi.astype(F32)).astype(BF)


def dot(a, b):
    return jnp.dot(a, b, preferred_element_type=F32)


def dot_t(a, b):
    return lax.dot_general(a, b, (((1,), (1,)), ((), ())), preferred_element_type=F32)


def t_dot(a, b):
    return lax.dot_general(a, b, (((0,), (0,)), ((), ())), preferred_element_type=F32)


def fold(m):
    return m[0:32] + m[32:64] + m[64:96] + m[96:128]


def kernel(
    tok_h, q_h, k_h, wv_in, wo_in, cot_h,
    out_h, gtok_h, gq_h, gk_h, gwv_o, gwo_o,
    local, tok, q_in, k_in, cot, out_o, gtok_o, gq_o, gk_o, sems, wv, wo, wvp, wop, tokp, tok_t, cotp, qp, kp, val, attf, denf, att_h, att_p, att_t,
    ghp, gvp, gqp, gkp, part1, part2, sib1, sib2, row1, row2, tot1, tot2,
    rs_v, rs_o, fin_v, fin_o, *slots,
):
    ins = [
        pltpu.make_async_copy(a, b, local.at[i])
        for i, (a, b) in enumerate(((tok_h, tok), (q_h, q_in), (k_h, k_in), (cot_h, cot)))
    ]
    for cp in ins:
        cp.start()
    leaving = []

    def leave(src, dst):
        cp = pltpu.make_async_copy(src, dst, local.at[4 + len(leaving)])
        cp.start()
        leaving.append(cp)

    me = Place()
    wire = Wire(sems)
    per = [len(scatter_slots(o)) for o in range(3)]
    cut = [0]
    for n in per * 2:
        cut.append(cut[-1] + n)
    slot_sets = [slots[cut[i] : cut[i + 1]] for i in range(6)]

    wv_t = wv.reshape(2, 16, 48, 16, 128)
    wo_t = wo.reshape(2, 16, 48, 16, 128)
    shard = me.xh * 8 + me.z
    wvp[...] = jnp.zeros_like(wvp)
    wvp[0:140, 0:1120] = wv_in[...]
    for l in range(5):
        slab = wvp[:, pl.ds(pl.multiple_of((5 * me.c + l) * 128, 128), 128)]
        wv_t[me.c, shard, 9 * l : 9 * l + 9] = slab.reshape(9, 16, 128)
    wv_t[me.c, shard, 45:48] = jnp.zeros((3, 16, 128), BF)
    wop[...] = jnp.zeros_like(wop)
    wop[0:70, 0:2240] = wo_in[...]
    for l in range(9):
        slab = wop[:, pl.ds(pl.multiple_of((9 * me.c + l) * 128, 128), 128)]
        wo_t[me.c, shard, 5 * l : 5 * l + 5] = slab.reshape(5, 16, 128)
    wo_t[me.c, shard, 45:48] = jnp.zeros((3, 16, 128), BF)

    peers = [me.peer("x", k) for k in (1, 2, 3)] + [me.peer("y", k) for k in (1, 2, 3)]
    peers += [me.peer("z", k) for k in range(1, 8)] + [me.sibling()]
    peers += [me.row_peer(dy, 1) for dy in (1, 2, 3)]
    peers += [me.row_peer(dy, dx, 1 - me.c) for dy, dx in PAIRS]
    barrier = pltpu.get_barrier_semaphore()
    for dev in peers:
        pl.semaphore_signal(barrier, inc=1, device_id=dev, device_id_type=MESH)
    pl.semaphore_wait(barrier, len(peers))

    a0 = [gather(wire, me, wv, 0, t) for t in range(2)]
    b0 = [gather(wire, me, wo, 0, t) for t in range(2)]
    a1, a2, b1, b2 = [[gather(wire, me, w, o)] for w in (wv, wo) for o in (1, 2)]

    def go(*order):
        for g in order:
            step(g)

    go(a1, a2, a0)
    go(b1, b2, a0)

    for cp in ins:
        cp.wait()
    tokp[...] = jnp.zeros_like(tokp)
    for i in range(16):
        tokp[:, 144 * i : 144 * i + 140] = tok[:, 140 * i : 140 * i + 140]
    go(a1, a2, b1, b2, a0)
    qp[...] = jnp.zeros_like(qp)
    qp[:, 0:1120] = q_in[...]
    kp[...] = jnp.zeros_like(kp)
    kp[:, 0:1120] = k_in[...]
    part1[...] = jnp.zeros_like(part1)
    part2[...] = jnp.zeros_like(part2)
    go(a1, a2, a0, b0)
    att_p[...] = jnp.zeros_like(att_p)
    gvp[me.c] = jnp.zeros((128, 1280), BF)
    cotp[me.c] = jnp.zeros((128, 2304), BF)
    cotp[me.c, :, 0:2240] = cot[...]
    go(a0)
    for i in range(9):
        tok_t[me.c, 256 * i : 256 * i + 256] = tokp[:, 256 * i : 256 * i + 256].T
    rsv_t = rs_v.reshape(16, 48, 16, 128)
    rso_t = rs_o.reshape(16, 48, 16, 128)
    rsv_t[:, 45:48] = jnp.zeros((16, 3, 16, 128), BF)
    rso_t[:, 45:48] = jnp.zeros((16, 3, 16, 128), BF)
    ghp[...] = jnp.zeros_like(ghp)
    go(a1, a2, a0, b0, b1, b2, a1, a2)
    go(a0, a1, a2)
    ex_cot = wire.send(cotp.at[me.c], cotp.at[me.c], me.sibling())
    ex_tok = wire.send(tok_t.at[me.c], tok_t.at[me.c], me.sibling())

    row = lax.broadcasted_iota(jnp.int32, (128, 128), 0) // 32
    col = lax.broadcasted_iota(jnp.int32, (128, 128), 1) // 32
    heads = (row == col).astype(F32)
    heads_b = heads.astype(BF)

    for group in ((0, 1), (2, 3), (4,), (5, 6), (7, 8)):
        acc = None
        for h in range(2):
            slab = jnp.concatenate(
                [
                    wv_t[s // 5, 8 * h : 8 * h + 8, 9 * (s % 5) : 9 * (s % 5) + 9].reshape(1152, 128)
                    for s in group
                ],
                axis=1,
            )
            part = dot(tokp[:, 1152 * h : 1152 * h + 1152], slab)
            acc = part if acc is None else acc + part
        val[:, 128 * group[0] : 128 * (group[-1] + 1)] = acc.astype(BF)
        if group[0] == 2:
            step(b0)

    def lanes_of(g):
        return pl.ds(pl.multiple_of(g * 128, 128), 128)

    def put(ref, img, g, m, line):
        ref[img, pl.ds(5 * g, 4)] = fold(m * heads).reshape(4, 8, 128)
        ref[img, 5 * g + 4] = jnp.broadcast_to(line, (8, 128))

    def take(ref, img, g):
        m = ref[img, pl.ds(5 * g, 4)].reshape(32, 128)
        m = jnp.concatenate([m, m, m, m], axis=0) * heads
        return m, ref[img, 5 * g + 4][0:1]

    for img in range(2):
        rows = slice(64 * img, 64 * img + 64)

        def state(g, carry, img=img, rows=rows):
            ln = lanes_of(g)
            kf = jnp.maximum(kp[rows, ln], 0)
            line = jnp.sum(kf.astype(F32), axis=0, keepdims=True)
            put(part1, img, g, t_dot(kf, val[rows, ln]), line)
            return carry

        lax.fori_loop(0, 9, state, 0, unroll=3)

    s1 = [seq_sum(wire, me, part1, sib1, row1, tot1)]
    go(s1, b0, s1, s1, b1, b2, b0, s1, s1)

    for img in range(2):
        rows = slice(64 * img, 64 * img + 64)

        def attend(g, carry, img=img, rows=rows):
            ln = lanes_of(g)
            qf = jnp.maximum(qp[rows, ln], 0)
            kv, kt = take(tot1, img, g)
            hi, lo = split(kv)
            numer = dot(qf, hi) + dot(qf, lo)
            hi, lo = split(qf.astype(F32) * kt)
            denom = dot(hi, heads_b) + dot(lo, heads_b) + 1.0
            ratio = numer / denom
            denf[rows, ln] = denom
            attf[rows, ln] = ratio
            att_h[rows, ln] = ratio.astype(BF)
            return carry

        lax.fori_loop(0, 9, attend, 0, unroll=3)
    for i in range(16):
        att_p[:, 80 * i : 80 * i + 70] = att_h[:, 70 * i : 70 * i + 70]
    for i in range(5):
        att_t[me.c, 256 * i : 256 * i + 256] = att_p[:, 256 * i : 256 * i + 256].T
    ex_att = wire.send(att_t.at[me.c], att_t.at[me.c], me.sibling())
    while b0 or b1 or b2:
        step(b1)
        step(b2)
        step(b0)

    ex_cot.wait_recv()
    ex_att.wait_recv()

    cot_half = pl.ds(pl.multiple_of(me.c * 1152, 128), 1152)

    def out_term(i, carry):
        a = jnp.concatenate([att_t[s, pl.ds(pl.multiple_of(160 * i, 32), 160)] for s in (0, 1)], axis=1)
        b = jnp.concatenate([cotp[0, :, cot_half], cotp[1, :, cot_half]], axis=0)
        m = dot(a, b).astype(BF)
        for l in range(9):
            rso_t[pl.ds(2 * i, 2), 5 * l : 5 * l + 5] = m[:, 128 * l : 128 * l + 128].reshape(2, 5, 16, 128)
        return carry

    lax.fori_loop(0, 8, out_term, 0)
    so = [scatter(wire, me, rs_o, o, slot_sets[o], fin_o) for o in range(3)]
    so_ring = so[:1]
    step(so)

    def out_rows(i, n):
        return jnp.concatenate(
            [
                wo_t[s // 9, i : i + n, 5 * (s % 9) : 5 * (s % 9) + 5].reshape(80 * n, 128)
                for s in range(18)
            ],
            axis=1,
        )

    for i in range(4):
        gh = dot_t(cotp[me.c], out_rows(4 * i, 4))
        for j in range(4):
            at = 70 * (4 * i + j)
            ghp[:, at : at + 70] = gh[:, 80 * j : 80 * j + 70]
        if i == 2:
            step(so_ring)

    for img in range(2):
        rows = slice(64 * img, 64 * img + 64)

        def grads(g, carry, img=img, rows=rows):
            ln = lanes_of(g)
            q = qp[rows, ln]
            qf = jnp.maximum(q, 0)
            kv, kt = take(tot1, img, g)
            kv_hi, kv_lo = split(kv)
            gn = ghp[rows, ln] / denf[rows, ln]
            hi, lo = split(gn * attf[rows, ln])
            gd = -(dot(hi, heads_b) + dot(lo, heads_b))
            hi, lo = split(gn)
            part = dot_t(hi, kv_hi) + dot_t(lo, kv_hi) + dot_t(hi, kv_lo) + gd * kt
            gqp[rows, ln] = jnp.where(q > 0, part, 0.0).astype(BF)
            line = jnp.sum(qf.astype(F32) * gd, axis=0, keepdims=True)
            put(part2, img, g, t_dot(qf, hi) + t_dot(qf, lo), line)
            return carry

        lax.fori_loop(0, 9, grads, 0, unroll=3)

    s2 = [seq_sum(wire, me, part2, sib2, row2, tot2)]
    step(s2)
    gq_o[...] = gqp[:, 0:1120]
    leave(gq_o, gq_h)
    step(so_ring)
    step(s2)

    step(so_ring)
    step(s2)
    for i in range(9):
        slab = jnp.concatenate(
            [
                wo_t[s // 9, :, 5 * (s % 9) : 5 * (s % 9) + 5].reshape(1280, 128)
                for s in (2 * i, 2 * i + 1)
            ],
            axis=1,
        )
        width = min(256, 2240 - 256 * i)
        out_o[:, 256 * i : 256 * i + width] = dot(att_p[...], slab).astype(BF)[:, 0:width]
    step(so)
    while s2:
        step(s2)

    for img in range(2):
        rows = slice(64 * img, 64 * img + 64)

        def last_grads(g, carry, img=img, rows=rows):
            ln = lanes_of(g)
            k = kp[rows, ln]
            kf = jnp.maximum(k, 0)
            gs, gt = take(tot2, img, g)
            hi, lo = split(gs)
            gvp[me.c, rows, ln] = (dot(kf, hi) + dot(kf, lo)).astype(BF)
            v = val[rows, ln]
            part = dot_t(v, hi) + dot_t(v, lo) + gt
            gkp[rows, ln] = jnp.where(k > 0, part, 0.0).astype(BF)
            return carry

        lax.fori_loop(0, 9, last_grads, 0, unroll=3)
    ex_gv = wire.send(gvp.at[me.c], gvp.at[me.c], me.sibling())
    step(so)
    gk_o[...] = gkp[:, 0:1120]
    leave(gk_o, gk_h)
    leave(out_o, out_h)
    ex_tok.wait_recv()
    ex_gv.wait_recv()

    gv_half = pl.ds(pl.multiple_of(me.c * 640, 128), 640)

    def value_term(i, carry):
        a = jnp.concatenate([tok_t[s, pl.ds(pl.multiple_of(288 * i, 32), 288)] for s in (0, 1)], axis=1)
        b = jnp.concatenate([gvp[0, :, gv_half], gvp[1, :, gv_half]], axis=0)
        m = dot(a, b).astype(BF)
        for l in range(5):
            rsv_t[pl.ds(2 * i, 2), 9 * l : 9 * l + 9] = m[:, 128 * l : 128 * l + 128].reshape(2, 9, 16, 128)
        return carry

    lax.fori_loop(0, 8, value_term, 0)
    sv = [scatter(wire, me, rs_v, o, slot_sets[3 + o], fin_v) for o in range(3)]
    sv_ring, sv_direct = sv[:1], sv[1:]
    go(sv_direct, sv_ring)
    while so:
        step(so)
    eo = [spread(wire, me, fin_o)]
    step(eo)

    for i in range(4):
        w = jnp.concatenate(
            [
                wv_t[s // 5, 4 * i : 4 * i + 4, 9 * (s % 5) : 9 * (s % 5) + 9].reshape(576, 128)
                for s in range(9)
            ],
            axis=1,
        )
        gt = dot_t(gvp[me.c, :, 0:1152], w).astype(BF)
        for j in range(4):
            at = 140 * (4 * i + j)
            gtok_o[:, at : at + 140] = gt[:, 144 * j : 144 * j + 140]
        if i < 3:
            step(sv_ring)
    go(sv_direct, sv_ring, eo)
    while sv_direct or sv_ring:
        go(sv_direct, sv_ring)
    leave(gtok_o, gtok_h)
    ends = [deliver(wire, me, fin_v)] + eo
    while ends:
        step(ends)
    seq = me.p * 2 + me.c
    fin_vt = fin_v.reshape(2, 48, 16, 128)
    fin_ot = fin_o.reshape(2, 48, 16, 128)

    def slab_of(ref, s, per_core, height):
        tiles = ref[lax.div(s, per_core), pl.ds(lax.rem(s, per_core) * height, height)]
        return tiles.reshape(height * 16, 128)

    first = lax.div(70 * seq, 128)
    shift = 70 * seq - 128 * first
    m = jnp.concatenate([slab_of(fin_vt, jnp.minimum(first + j, 8), 5, 9) for j in range(2)], axis=1)
    gwv_o[...] = pltpu.roll(m, lax.rem(256 - shift, 256), 1)[0:140, 0:70]
    first = lax.div(140 * seq, 128)
    shift = 140 * seq - 128 * first
    m = jnp.concatenate([slab_of(fin_ot, jnp.minimum(first + j, 17), 9, 5) for j in range(3)], axis=1)
    gwo_o[...] = pltpu.roll(m, lax.rem(384 - shift, 384), 1)[0:70, 0:140]
    wire.drain()
    for cp in leaving:
        cp.wait()


def hand_over(*refs):
    for i in range(6):
        refs[6 + i][...] = refs[i][...]


def body(tokens, q_raw, k_raw, w_value, w_out, cotangent):
    shape = jax.ShapeDtypeStruct
    weight = VM((2, 2, 8, 4, 2, 3, 2, 16, 128), BF)
    partial = VM((2, 8, 4, 2, 3, 2, 16, 128), BF)
    state = VM((2, 48, 8, 128), F32)
    final = VM((2, 8, 3, 2, 16, 128), F32)
    slots = [s for _ in range(2) for o in range(3) for s in scatter_slots(o)]
    outs = pl.pallas_call(
        kernel,
        out_shape=(
            shape((128, 2240), BF),
            shape((128, 2240), BF),
            shape((128, 1120), BF),
            shape((128, 1120), BF),
            shape((140, 70), F32),
            shape((70, 140), F32),
        ),
        in_specs=[pl.BlockSpec(memory_space=m) for m in (pl.ANY, pl.ANY, pl.ANY, VM, VM, pl.ANY)],
        out_specs=tuple(
            pl.BlockSpec(memory_space=m) for m in (pl.ANY, pl.ANY, pl.ANY, pl.ANY, VM, VM)
        ),
        scratch_shapes=[
            pltpu.SemaphoreType.DMA((8,)),
            VM((128, 2240), BF),
            VM((128, 1120), BF),
            VM((128, 1120), BF),
            VM((128, 2240), BF),
            VM((128, 2240), BF),
            VM((128, 2240), BF),
            VM((128, 1120), BF),
            VM((128, 1120), BF),
            pltpu.SemaphoreType.DMA((2, N_SEMS)),
            weight,
            weight,
            VM((144, 1408), BF),
            VM((80, 2432), BF),
            VM((128, 2304), BF),
            VM((2, 2304, 128), BF),
            VM((2, 128, 2304), BF),
            VM((128, 1152), BF),
            VM((128, 1152), BF),
            VM((128, 1152), BF),
            VM((128, 1152), F32),
            VM((128, 1152), F32),
            VM((128, 1152), BF),
            VM((128, 1280), BF),
            VM((2, 1280, 128), BF),
            VM((128, 1152), F32),
            VM((2, 128, 1280), BF),
            VM((128, 1152), BF),
            VM((128, 1152), BF),
            state,
            state,
            VM((48, 8, 128), F32),
            VM((48, 8, 128), F32),
            VM((7, 6, 8, 128), F32),
            VM((7, 6, 8, 128), F32),
            state,
            state,
            partial,
            partial,
            final,
            final,
            *slots,
        ],
        compiler_params=pltpu.CompilerParams(
            collective_id=0, has_side_effects=True, vmem_limit_bytes=60 * 2**20
        ),
    )(
        tokens.reshape(128, 2240),
        q_raw.reshape(128, 1120),
        k_raw.reshape(128, 1120),
        w_value,
        w_out,
        cotangent.reshape(128, 2240),
    )
    outs = pl.pallas_call(
        hand_over,
        out_shape=tuple(shape(o.shape, o.dtype) for o in outs),
        in_specs=[pl.BlockSpec(memory_space=VM)] * 6,
        out_specs=(pl.BlockSpec(memory_space=VM),) * 6,
    )(*outs)
    return (
        outs[0].reshape(2, 64, 2240),
        outs[1].reshape(2, 64, 2240),
        outs[2].reshape(2, 64, 1120),
        outs[3].reshape(2, 64, 1120),
        outs[4],
        outs[5],
    )


def solution(mesh):
    rows = P("dp", "seq", None)
    return jax.shard_map(
        body,
        mesh=mesh,
        in_specs=(rows, rows, rows, P("dp", None), P("dp", None), rows),
        out_specs=(rows, rows, rows, rows, P("dp", "seq"), P("dp", "seq")),
        check_vma=False,
    )
```

```python
import jax
import jax.numpy as jnp
from jax import lax
from jax.experimental import pallas as pl
from jax.experimental.pallas import tpu as pltpu
from jax.sharding import PartitionSpec as P

BF = jnp.bfloat16
F32 = jnp.float32
MESH = pl.DeviceIdType.MESH
VM = pltpu.VMEM
SIZE = {"x": 4, "y": 4, "z": 8}
SCATTER = (("z", "x", "y"), ("x", "y", "z"), ("y", "x", "z"))
PAIRS = ((0, 1), (1, 0), (1, 1), (2, 0), (2, 1), (3, 0), (3, 1))
N_SEMS = 320


class Place:
    def __init__(self):
        dp = lax.axis_index("dp")
        seq = lax.axis_index("seq")
        self.z = lax.rem(dp, 8)
        self.y = lax.div(seq, 4)
        self.xl = lax.rem(lax.div(seq, 2), 2)
        self.c = lax.rem(seq, 2)
        self.xh = lax.div(dp, 8)
        self.x = self.xh * 2 + self.xl
        self.p = self.y * 2 + self.xl

    def step(self, d, k):
        return lax.rem(getattr(self, d) + (k % SIZE[d]), SIZE[d])

    def dev(self, x=None, y=None, z=None, c=None):
        x = self.x if x is None else x
        y = self.y if y is None else y
        z = self.z if z is None else z
        c = self.c if c is None else c
        return (lax.div(x, 2) * 8 + z, (y * 2 + lax.rem(x, 2)) * 2 + c)

    def peer(self, d, k):
        return self.dev(**{d: self.step(d, k)})

    def sibling(self):
        return self.dev(c=1 - self.c)

    def row_peer(self, dy, dx, c=None):
        xl = lax.rem(self.xl + dx, 2)
        return self.dev(y=self.step("y", dy), x=self.x - self.xl + xl, c=c)

    def index(self, o, open_, d, b, half=None):
        co = {"x": self.x, "y": self.y, "z": self.z}
        for e in open_:
            co[e] = None
        co[d] = b
        every = slice(None)
        x = co["x"]
        xh, xl = (every, every) if x is None else (lax.div(x, 2), lax.rem(x, 2))
        z = every if co["z"] is None else co["z"]
        y = every if co["y"] is None else co["y"]
        out = (xh, z, y, xl, o)
        return out if half is None else out + (half,)


class Wire:
    def __init__(self, sems):
        self.sems = sems
        self.started = []

    def send(self, src, dst, dev):
        k = len(self.started)
        cp = pltpu.make_async_remote_copy(
            src_ref=src,
            dst_ref=dst,
            send_sem=self.sems.at[0, k],
            recv_sem=self.sems.at[1, k],
            device_id=dev,
            device_id_type=MESH,
        )
        cp.start()
        self.started.append(cp)
        return cp

    def drain(self):
        for cp in self.started:
            cp.wait_send()


def gather(wire, me, buf, o, tile=None):
    sib = []

    def share(ref):
        sib.append(wire.send(ref, ref, me.sibling()))

    def piece(xh=None, z=None, y=None, xl=None, half=None):
        every = slice(None)
        i = (me.c,) + tuple(every if v is None else v for v in (xh, z, y, xl)) + (o,)
        return buf.at[i if half is None else i + (half,)]

    def direct(d, ref):
        cps = [wire.send(ref, ref, me.peer(d, k)) for k in range(1, SIZE[d])]
        yield
        for cp in cps:
            cp.wait_recv()

    def ring(d, block):
        share(block(getattr(me, d)))
        steps = SIZE[d] // 2
        for s in range(1, steps + 1):
            hp, hm = (0, 1) if s == steps else (None, None)
            fp = block(me.step(d, -(s - 1)), hp)
            fm = block(me.step(d, s - 1), hm)
            plus = wire.send(fp, fp, me.peer(d, 1))
            minus = wire.send(fm, fm, me.peer(d, -1))
            yield
            plus.wait_recv()
            minus.wait_recv()
            share(block(me.step(d, -s), hp))
            share(block(me.step(d, s), hm))

    if o == 0:
        ref = piece(xh=me.xh, z=me.z, half=tile)
        cp = wire.send(ref, ref, me.dev(x=3 - me.x))
        yield
        cp.wait_recv()
        share(piece(z=me.z, half=tile))
        for s in range(1, 5):
            cps = []
            for sign in (1, -1) if s < 4 else ((1, -1)[tile],):
                ref = piece(z=me.step("z", -sign * (s - 1)), half=tile)
                cps.append((sign, wire.send(ref, ref, me.peer("z", sign))))
            yield
            for sign, cp in cps:
                cp.wait_recv()
                share(piece(z=me.step("z", -sign * s), half=tile))
    elif o == 1:
        yield from direct("z", piece(me.xh, me.z, me.y, me.xl))
        yield from direct("y", piece(xh=me.xh, y=me.y, xl=me.xl))
        yield from ring(
            "x", lambda b, h=None: piece(xh=lax.div(b, 2), xl=lax.rem(b, 2), half=h)
        )
    else:
        yield from direct("z", piece(me.xh, me.z, me.y, me.xl))
        yield from direct("x", piece(xh=me.xh, y=me.y, xl=me.xl))
        yield from ring("y", lambda b, h=None: piece(y=b, half=h))
    yield
    for cp in sib:
        cp.wait_recv()


def scatter(wire, me, buf, o, rx, fin):
    rx = iter(rx)
    dims = SCATTER[o]
    for n, d in enumerate(dims):
        open_ = dims[n + 1 :]
        last = n == 2

        def at(k, half=None):
            return me.index(o, open_, d, me.step(d, k), half)

        own = at(0)
        if d != "z" or n:
            slots = [next(rx) for _ in range(1, SIZE[d])]
            cps = [
                wire.send(buf.at[at(k)], slots[k - 1], me.peer(d, k))
                for k in range(1, SIZE[d])
            ]
            yield
            acc = buf[own].astype(F32)
            for cp, slot in zip(cps, slots):
                cp.wait_recv()
                acc = acc + slot[...].astype(F32)
        else:
            up = [next(rx) for _ in range(4)]
            down = [next(rx) for _ in range(4)]
            for s in range(1, 5):
                k = 5 - s
                hp, hm = (0, 1) if s == 1 else (None, None)
                if s > 1:
                    plus.wait_recv()
                    minus.wait_recv()
                    for sign, slot, half in ((1, up[s - 2], 0), (-1, down[s - 2], 1)):
                        i = at(sign * k, half if s == 2 else None)
                        buf[i] = (buf[i].astype(F32) + slot[...].astype(F32)).astype(BF)
                plus = wire.send(buf.at[at(k, hp)], up[s - 1], me.peer(d, 1))
                minus = wire.send(buf.at[at(-k, hm)], down[s - 1], me.peer(d, -1))
                yield
            plus.wait_recv()
            minus.wait_recv()
            acc = buf[own].astype(F32) + up[3][...].astype(F32) + down[3][...].astype(F32)
        if last:
            fin[me.c, me.p, o] = acc
        else:
            buf[own] = acc.astype(BF)


def scatter_slots(o):
    dims = SCATTER[o]
    out = []
    for n, d in enumerate(dims):
        open_ = dims[n + 1 :]
        shape = ()
        if "x" in open_:
            shape += (2,)
        if "z" in open_:
            shape += (8,)
        if "y" in open_:
            shape += (4,)
        if "x" in open_:
            shape += (2,)
        tile = (16, 128)
        if d != "z" or n:
            out += [VM(shape + (2,) + tile, BF)] * (SIZE[d] - 1)
        else:
            out += ([VM(shape + tile, BF)] + [VM(shape + (2,) + tile, BF)] * 3) * 2
    return out


def spread(wire, me, fin):
    mine = fin.at[me.c, me.p]
    cps = [wire.send(mine, mine, me.row_peer(dy, dx)) for dy, dx in PAIRS]
    yield
    for cp in cps:
        cp.wait_recv()
    half = fin.at[me.c]
    cp = wire.send(half, half, me.sibling())
    yield
    cp.wait_recv()


def span(c, p, div):
    first = 5 * c + div(2 * p, 3)
    final = 5 * c + div(6 * p + 5, 9)
    return div(128 * first, 70), div(128 * final + 127, 70)


def deliver(wire, me, fin):
    base = N_SEMS - 16
    seq = me.p * 2 + me.c
    mine = fin.at[me.c, me.p]
    first, final = span(me.c, me.p, lax.div)
    ends = []
    for e in range(5):
        to = first + e
        cp = pltpu.make_async_remote_copy(
            src_ref=mine,
            dst_ref=mine,
            send_sem=wire.sems.at[0, base + e],
            recv_sem=wire.sems.at[1, base + me.c * 8 + me.p],
            device_id=(me.xh * 8 + me.z, jnp.minimum(to, 15)),
            device_id_type=MESH,
        )
        used = (to <= final) & (to <= 15) & (to != seq)
        pl.when(used)(cp.start)
        ends.append((used, cp))
    yield
    for c in range(2):
        for p in range(8):
            lo, hi = span(c, p, lambda a, b: a // b)
            if lo > 15:
                continue
            used = (seq >= lo) & (seq <= hi) & (seq != 2 * p + c)
            cp = pltpu.make_async_remote_copy(
                src_ref=fin.at[c, p],
                dst_ref=fin.at[c, p],
                send_sem=wire.sems.at[0, base + 5],
                recv_sem=wire.sems.at[1, base + c * 8 + p],
                device_id=me.sibling(),
                device_id_type=MESH,
            )
            pl.when(used)(cp.wait_recv)
    for used, cp in ends:
        pl.when(used)(cp.wait_send)


def seq_sum(wire, me, part, from_sib, from_row, total):
    cp = wire.send(part.at[1 - me.c], from_sib, me.sibling())
    yield
    cp.wait_recv()
    part[me.c] = part[me.c] + from_sib[...]
    cps = []
    for n, (dy, dx) in enumerate(PAIRS):
        p = me.step("y", dy) * 2 + lax.rem(me.xl + dx, 2)
        cps.append(
            wire.send(part.at[me.c, pl.ds(6 * p, 6)], from_row.at[n], me.row_peer(dy, dx))
        )
    yield
    acc = part[me.c, pl.ds(6 * me.p, 6)]
    for n, cp in enumerate(cps):
        cp.wait_recv()
        acc = acc + from_row[n]
    total[me.c, pl.ds(6 * me.p, 6)] = acc
    mine = total.at[me.c, pl.ds(6 * me.p, 6)]
    cps = [wire.send(mine, mine, me.row_peer(dy, dx)) for dy, dx in PAIRS]
    yield
    for cp in cps:
        cp.wait_recv()
    half = total.at[me.c]
    cp = wire.send(half, half, me.sibling())
    yield
    cp.wait_recv()


def step(gens):
    for g in list(gens):
        try:
            next(g)
        except StopIteration:
            gens.remove(g)


def split(a):
    hi = a.astype(BF)
    return hi, (a - hi.astype(F32)).astype(BF)


def dot(a, b):
    return jnp.dot(a, b, preferred_element_type=F32)


def dot_t(a, b):
    return lax.dot_general(a, b, (((1,), (1,)), ((), ())), preferred_element_type=F32)


def t_dot(a, b):
    return lax.dot_general(a, b, (((0,), (0,)), ((), ())), preferred_element_type=F32)


def fold(m):
    return m[0:32] + m[32:64] + m[64:96] + m[96:128]


def kernel(
    tok_h, q_h, k_h, wv_in, wo_in, cot_h,
    out_h, gtok_h, gq_h, gk_h, gwv_o, gwo_o,
    local, tok, q_in, k_in, cot, out_o, gtok_o, gq_o, gk_o, sems, wv, wo, wvp, wop, tokp, tok_t, cotp, qp, kp, val, attf, denf, att_h, att_p, att_t,
    ghp, gvp, gqp, gkp, part1, part2, sib1, sib2, row1, row2, tot1, tot2,
    rs_v, rs_o, fin_v, fin_o, *slots,
):
    ins = [
        pltpu.make_async_copy(a, b, local.at[i])
        for i, (a, b) in enumerate(((tok_h, tok), (q_h, q_in), (k_h, k_in), (cot_h, cot)))
    ]
    for cp in ins:
        cp.start()
    leaving = []

    def leave(src, dst):
        cp = pltpu.make_async_copy(src, dst, local.at[4 + len(leaving)])
        cp.start()
        leaving.append(cp)

    me = Place()
    wire = Wire(sems)
    per = [len(scatter_slots(o)) for o in range(3)]
    cut = [0]
    for n in per * 2:
        cut.append(cut[-1] + n)
    slot_sets = [slots[cut[i] : cut[i + 1]] for i in range(6)]

    wv_t = wv.reshape(2, 16, 48, 16, 128)
    wo_t = wo.reshape(2, 16, 48, 16, 128)
    shard = me.xh * 8 + me.z
    wvp[...] = jnp.zeros_like(wvp)
    wvp[0:140, 0:1120] = wv_in[...]
    for l in range(5):
        slab = wvp[:, pl.ds(pl.multiple_of((5 * me.c + l) * 128, 128), 128)]
        wv_t[me.c, shard, 9 * l : 9 * l + 9] = slab.reshape(9, 16, 128)
    wv_t[me.c, shard, 45:48] = jnp.zeros((3, 16, 128), BF)
    wop[...] = jnp.zeros_like(wop)
    wop[0:70, 0:2240] = wo_in[...]
    for l in range(9):
        slab = wop[:, pl.ds(pl.multiple_of((9 * me.c + l) * 128, 128), 128)]
        wo_t[me.c, shard, 5 * l : 5 * l + 5] = slab.reshape(5, 16, 128)
    wo_t[me.c, shard, 45:48] = jnp.zeros((3, 16, 128), BF)

    peers = [me.peer("x", k) for k in (1, 2, 3)] + [me.peer("y", k) for k in (1, 2, 3)]
    peers += [me.peer("z", k) for k in range(1, 8)] + [me.sibling()]
    peers += [me.row_peer(dy, 1) for dy in (1, 2, 3)]
    peers += [me.row_peer(dy, dx, 1 - me.c) for dy, dx in PAIRS]
    barrier = pltpu.get_barrier_semaphore()
    for dev in peers:
        pl.semaphore_signal(barrier, inc=1, device_id=dev, device_id_type=MESH)
    pl.semaphore_wait(barrier, len(peers))

    a0 = [gather(wire, me, wv, 0, t) for t in range(2)]
    b0 = [gather(wire, me, wo, 0, t) for t in range(2)]
    a1, a2, b1, b2 = [[gather(wire, me, w, o)] for w in (wv, wo) for o in (1, 2)]

    def go(*order):
        for g in order:
            step(g)

    go(a1, a2, a0)
    go(b1, b2, a0)

    for cp in ins:
        cp.wait()
    tokp[...] = jnp.zeros_like(tokp)
    for i in range(16):
        tokp[:, 144 * i : 144 * i + 140] = tok[:, 140 * i : 140 * i + 140]
    go(a1, a2, b1, b2, a0)
    qp[...] = jnp.zeros_like(qp)
    qp[:, 0:1120] = q_in[...]
    kp[...] = jnp.zeros_like(kp)
    kp[:, 0:1120] = k_in[...]
    part1[...] = jnp.zeros_like(part1)
    part2[...] = jnp.zeros_like(part2)
    go(a1, a2, a0, b0)
    att_p[...] = jnp.zeros_like(att_p)
    gvp[me.c] = jnp.zeros((128, 1280), BF)
    cotp[me.c] = jnp.zeros((128, 2304), BF)
    cotp[me.c, :, 0:2240] = cot[...]
    go(a0)
    for i in range(9):
        tok_t[me.c, 256 * i : 256 * i + 256] = tokp[:, 256 * i : 256 * i + 256].T
    rsv_t = rs_v.reshape(16, 48, 16, 128)
    rso_t = rs_o.reshape(16, 48, 16, 128)
    rsv_t[:, 45:48] = jnp.zeros((16, 3, 16, 128), BF)
    rso_t[:, 45:48] = jnp.zeros((16, 3, 16, 128), BF)
    ghp[...] = jnp.zeros_like(ghp)
    go(a1, a2, a0, b0, b1, b2, a1, a2)
    go(a0, a1, a2)
    ex_cot = wire.send(cotp.at[me.c], cotp.at[me.c], me.sibling())
    ex_tok = wire.send(tok_t.at[me.c], tok_t.at[me.c], me.sibling())

    row = lax.broadcasted_iota(jnp.int32, (128, 128), 0) // 32
    col = lax.broadcasted_iota(jnp.int32, (128, 128), 1) // 32
    heads = (row == col).astype(F32)
    heads_b = heads.astype(BF)

    for group in ((0, 1), (2, 3), (4,), (5, 6), (7, 8)):
        acc = None
        for h in range(2):
            slab = jnp.concatenate(
                [
                    wv_t[s // 5, 8 * h : 8 * h + 8, 9 * (s % 5) : 9 * (s % 5) + 9].reshape(1152, 128)
                    for s in group
                ],
                axis=1,
            )
            part = dot(tokp[:, 1152 * h : 1152 * h + 1152], slab)
            acc = part if acc is None else acc + part
        val[:, 128 * group[0] : 128 * (group[-1] + 1)] = acc.astype(BF)
        if group[0] == 2:
            step(b0)

    def lanes_of(g):
        return pl.ds(pl.multiple_of(g * 128, 128), 128)

    def put(ref, img, g, m, line):
        ref[img, pl.ds(5 * g, 4)] = fold(m * heads).reshape(4, 8, 128)
        ref[img, 5 * g + 4] = jnp.broadcast_to(line, (8, 128))

    def take(ref, img, g):
        m = ref[img, pl.ds(5 * g, 4)].reshape(32, 128)
        m = jnp.concatenate([m, m, m, m], axis=0) * heads
        return m, ref[img, 5 * g + 4][0:1]

    for img in range(2):
        rows = slice(64 * img, 64 * img + 64)

        def state(g, carry, img=img, rows=rows):
            ln = lanes_of(g)
            kf = jnp.maximum(kp[rows, ln], 0)
            line = jnp.sum(kf.astype(F32), axis=0, keepdims=True)
            put(part1, img, g, t_dot(kf, val[rows, ln]), line)
            return carry

        lax.fori_loop(0, 9, state, 0, unroll=3)

    s1 = [seq_sum(wire, me, part1, sib1, row1, tot1)]
    go(s1, b0, s1, s1, b1, b2, b0, s1, s1)

    for img in range(2):
        rows = slice(64 * img, 64 * img + 64)

        def attend(g, carry, img=img, rows=rows):
            ln = lanes_of(g)
            qf = jnp.maximum(qp[rows, ln], 0)
            kv, kt = take(tot1, img, g)
            hi, lo = split(kv)
            numer = dot(qf, hi) + dot(qf, lo)
            hi, lo = split(qf.astype(F32) * kt)
            denom = dot(hi, heads_b) + dot(lo, heads_b) + 1.0
            ratio = numer / denom
            denf[rows, ln] = denom
            attf[rows, ln] = ratio
            att_h[rows, ln] = ratio.astype(BF)
            return carry

        lax.fori_loop(0, 9, attend, 0, unroll=3)
    for i in range(16):
        att_p[:, 80 * i : 80 * i + 70] = att_h[:, 70 * i : 70 * i + 70]
    for i in range(5):
        att_t[me.c, 256 * i : 256 * i + 256] = att_p[:, 256 * i : 256 * i + 256].T
    ex_att = wire.send(att_t.at[me.c], att_t.at[me.c], me.sibling())
    while b0 or b1 or b2:
        step(b1)
        step(b2)
        step(b0)

    ex_cot.wait_recv()
    ex_att.wait_recv()

    cot_half = pl.ds(pl.multiple_of(me.c * 1152, 128), 1152)

    def out_term(i, carry):
        a = jnp.concatenate([att_t[s, pl.ds(pl.multiple_of(160 * i, 32), 160)] for s in (0, 1)], axis=1)
        b = jnp.concatenate([cotp[0, :, cot_half], cotp[1, :, cot_half]], axis=0)
        m = dot(a, b).astype(BF)
        for l in range(9):
            rso_t[pl.ds(2 * i, 2), 5 * l : 5 * l + 5] = m[:, 128 * l : 128 * l + 128].reshape(2, 5, 16, 128)
        return carry

    lax.fori_loop(0, 8, out_term, 0)
    so = [scatter(wire, me, rs_o, o, slot_sets[o], fin_o) for o in range(3)]
    so_ring = so[:1]
    step(so)

    def out_rows(i, n):
        return jnp.concatenate(
            [
                wo_t[s // 9, i : i + n, 5 * (s % 9) : 5 * (s % 9) + 5].reshape(80 * n, 128)
                for s in range(18)
            ],
            axis=1,
        )

    for i in range(4):
        gh = dot_t(cotp[me.c], out_rows(4 * i, 4))
        for j in range(4):
            at = 70 * (4 * i + j)
            ghp[:, at : at + 70] = gh[:, 80 * j : 80 * j + 70]
        if i == 2:
            step(so_ring)

    for img in range(2):
        rows = slice(64 * img, 64 * img + 64)

        def grads(g, carry, img=img, rows=rows):
            ln = lanes_of(g)
            q = qp[rows, ln]
            qf = jnp.maximum(q, 0)
            kv, kt = take(tot1, img, g)
            kv_hi, kv_lo = split(kv)
            gn = ghp[rows, ln] / denf[rows, ln]
            hi, lo = split(gn * attf[rows, ln])
            gd = -(dot(hi, heads_b) + dot(lo, heads_b))
            hi, lo = split(gn)
            part = dot_t(hi, kv_hi) + dot_t(lo, kv_hi) + dot_t(hi, kv_lo) + gd * kt
            gqp[rows, ln] = jnp.where(q > 0, part, 0.0).astype(BF)
            line = jnp.sum(qf.astype(F32) * gd, axis=0, keepdims=True)
            put(part2, img, g, t_dot(qf, hi) + t_dot(qf, lo), line)
            return carry

        lax.fori_loop(0, 9, grads, 0, unroll=3)

    s2 = [seq_sum(wire, me, part2, sib2, row2, tot2)]
    step(s2)
    gq_o[...] = gqp[:, 0:1120]
    leave(gq_o, gq_h)
    step(so_ring)
    step(s2)

    step(so_ring)
    step(s2)
    for i in range(9):
        slab = jnp.concatenate(
            [
                wo_t[s // 9, :, 5 * (s % 9) : 5 * (s % 9) + 5].reshape(1280, 128)
                for s in (2 * i, 2 * i + 1)
            ],
            axis=1,
        )
        width = min(256, 2240 - 256 * i)
        out_o[:, 256 * i : 256 * i + width] = dot(att_p[...], slab).astype(BF)[:, 0:width]
    step(s2)
    go(so[1:], so_ring)
    while s2:
        step(s2)

    for img in range(2):
        rows = slice(64 * img, 64 * img + 64)

        def last_grads(g, carry, img=img, rows=rows):
            ln = lanes_of(g)
            k = kp[rows, ln]
            kf = jnp.maximum(k, 0)
            gs, gt = take(tot2, img, g)
            hi, lo = split(gs)
            gvp[me.c, rows, ln] = (dot(kf, hi) + dot(kf, lo)).astype(BF)
            v = val[rows, ln]
            part = dot_t(v, hi) + dot_t(v, lo) + gt
            gkp[rows, ln] = jnp.where(k > 0, part, 0.0).astype(BF)
            return carry

        lax.fori_loop(0, 9, last_grads, 0, unroll=3)
    ex_gv = wire.send(gvp.at[me.c], gvp.at[me.c], me.sibling())
    go(so[1:], so_ring)
    gk_o[...] = gkp[:, 0:1120]
    leave(gk_o, gk_h)
    leave(out_o, out_h)
    ex_tok.wait_recv()
    ex_gv.wait_recv()

    gv_half = pl.ds(pl.multiple_of(me.c * 640, 128), 640)

    def value_term(i, carry):
        a = jnp.concatenate([tok_t[s, pl.ds(pl.multiple_of(288 * i, 32), 288)] for s in (0, 1)], axis=1)
        b = jnp.concatenate([gvp[0, :, gv_half], gvp[1, :, gv_half]], axis=0)
        m = dot(a, b).astype(BF)
        for l in range(5):
            rsv_t[pl.ds(2 * i, 2), 9 * l : 9 * l + 9] = m[:, 128 * l : 128 * l + 128].reshape(2, 9, 16, 128)
        return carry

    lax.fori_loop(0, 8, value_term, 0)
    sv = [scatter(wire, me, rs_v, o, slot_sets[3 + o], fin_v) for o in range(3)]
    sv_ring, sv_direct = sv[:1], sv[1:]
    go(sv_direct, sv_ring)
    while so:
        step(so)
    eo = [spread(wire, me, fin_o)]
    step(eo)

    for i in range(4):
        w = jnp.concatenate(
            [
                wv_t[s // 5, 4 * i : 4 * i + 4, 9 * (s % 5) : 9 * (s % 5) + 9].reshape(576, 128)
                for s in range(9)
            ],
            axis=1,
        )
        gt = dot_t(gvp[me.c, :, 0:1152], w).astype(BF)
        for j in range(4):
            at = 140 * (4 * i + j)
            gtok_o[:, at : at + 140] = gt[:, 144 * j : 144 * j + 140]
        if i < 3:
            step(sv_ring)
    go(sv_direct, sv_ring, eo)
    while sv_direct or sv_ring:
        go(sv_direct, sv_ring)
    leave(gtok_o, gtok_h)
    ends = [deliver(wire, me, fin_v)] + eo
    while ends:
        step(ends)
    seq = me.p * 2 + me.c
    fin_vt = fin_v.reshape(2, 48, 16, 128)
    fin_ot = fin_o.reshape(2, 48, 16, 128)

    def slab_of(ref, s, per_core, height):
        tiles = ref[lax.div(s, per_core), pl.ds(lax.rem(s, per_core) * height, height)]
        return tiles.reshape(height * 16, 128)

    first = lax.div(70 * seq, 128)
    shift = 70 * seq - 128 * first
    m = jnp.concatenate([slab_of(fin_vt, jnp.minimum(first + j, 8), 5, 9) for j in range(2)], axis=1)
    gwv_o[...] = pltpu.roll(m, lax.rem(256 - shift, 256), 1)[0:140, 0:70]
    first = lax.div(140 * seq, 128)
    shift = 140 * seq - 128 * first
    m = jnp.concatenate([slab_of(fin_ot, jnp.minimum(first + j, 17), 9, 5) for j in range(3)], axis=1)
    gwo_o[...] = pltpu.roll(m, lax.rem(384 - shift, 384), 1)[0:70, 0:140]
    wire.drain()
    for cp in leaving:
        cp.wait()


def hand_over(*refs):
    for i in range(6):
        refs[6 + i][...] = refs[i][...]


def body(tokens, q_raw, k_raw, w_value, w_out, cotangent):
    shape = jax.ShapeDtypeStruct
    weight = VM((2, 2, 8, 4, 2, 3, 2, 16, 128), BF)
    partial = VM((2, 8, 4, 2, 3, 2, 16, 128), BF)
    state = VM((2, 48, 8, 128), F32)
    final = VM((2, 8, 3, 2, 16, 128), F32)
    slots = [s for _ in range(2) for o in range(3) for s in scatter_slots(o)]
    outs = pl.pallas_call(
        kernel,
        out_shape=(
            shape((128, 2240), BF),
            shape((128, 2240), BF),
            shape((128, 1120), BF),
            shape((128, 1120), BF),
            shape((140, 70), F32),
            shape((70, 140), F32),
        ),
        in_specs=[pl.BlockSpec(memory_space=m) for m in (pl.ANY, pl.ANY, pl.ANY, VM, VM, pl.ANY)],
        out_specs=tuple(
            pl.BlockSpec(memory_space=m) for m in (pl.ANY, pl.ANY, pl.ANY, pl.ANY, VM, VM)
        ),
        scratch_shapes=[
            pltpu.SemaphoreType.DMA((8,)),
            VM((128, 2240), BF),
            VM((128, 1120), BF),
            VM((128, 1120), BF),
            VM((128, 2240), BF),
            VM((128, 2240), BF),
            VM((128, 2240), BF),
            VM((128, 1120), BF),
            VM((128, 1120), BF),
            pltpu.SemaphoreType.DMA((2, N_SEMS)),
            weight,
            weight,
            VM((144, 1408), BF),
            VM((80, 2432), BF),
            VM((128, 2304), BF),
            VM((2, 2304, 128), BF),
            VM((2, 128, 2304), BF),
            VM((128, 1152), BF),
            VM((128, 1152), BF),
            VM((128, 1152), BF),
            VM((128, 1152), F32),
            VM((128, 1152), F32),
            VM((128, 1152), BF),
            VM((128, 1280), BF),
            VM((2, 1280, 128), BF),
            VM((128, 1152), F32),
            VM((2, 128, 1280), BF),
            VM((128, 1152), BF),
            VM((128, 1152), BF),
            state,
            state,
            VM((48, 8, 128), F32),
            VM((48, 8, 128), F32),
            VM((7, 6, 8, 128), F32),
            VM((7, 6, 8, 128), F32),
            state,
            state,
            partial,
            partial,
            final,
            final,
            *slots,
        ],
        compiler_params=pltpu.CompilerParams(
            collective_id=0, has_side_effects=True, vmem_limit_bytes=60 * 2**20
        ),
    )(
        tokens.reshape(128, 2240),
        q_raw.reshape(128, 1120),
        k_raw.reshape(128, 1120),
        w_value,
        w_out,
        cotangent.reshape(128, 2240),
    )
    outs = pl.pallas_call(
        hand_over,
        out_shape=tuple(shape(o.shape, o.dtype) for o in outs),
        in_specs=[pl.BlockSpec(memory_space=VM)] * 6,
        out_specs=(pl.BlockSpec(memory_space=VM),) * 6,
    )(*outs)
    return (
        outs[0].reshape(2, 64, 2240),
        outs[1].reshape(2, 64, 2240),
        outs[2].reshape(2, 64, 1120),
        outs[3].reshape(2, 64, 1120),
        outs[4],
        outs[5],
    )


def solution(mesh):
    rows = P("dp", "seq", None)
    return jax.shard_map(
        body,
        mesh=mesh,
        in_specs=(rows, rows, rows, P("dp", None), P("dp", None), rows),
        out_specs=(rows, rows, rows, rows, P("dp", "seq"), P("dp", "seq")),
        check_vma=False,
    )
```
